32 devices in a mesh: orient: 16 (over z, y, core), coef: 2 (over x).
Axes of the slice: x: 2, y: 2, z: 4, core: 2. Of those that a mesh axis runs over, the one named last changes fastest.
Arguments:
- volume: bfloat16 [16, 12, 128, 128], P('orient', 'coef'), may hold values from -6 to 6
- measured: float32 [16, 16, 64, 128], P('orient'), may hold values from -6 to 6
- basis_table: float32 [16, 64, 12], P(None, None, 'coef'), may hold values from -1.75 to 1.75
- angle_table: float32 [16], replicated, may hold values from -1.2 to 1.2
- angle_index: int32 [16], P('orient'), may hold values from 0 to 15, each once
- sector_map: int32 [16, 64], P('orient'), may hold values from 0 to 63, each once within a row
Outputs:
- gradient: float32 [16, 12, 128, 128], P('orient', 'coef')
- residual: float32 [16, 16, 64, 128], P('orient', None, 'coef')
The draws below stay inside these ranges and needn't reach their ends.
Inputs may be any that keep to these rules, and one draw needn't show every extreme that they name: `angle_index`: a permutation of the table orientations. `sector_map`: each row is a permutation of the 64 sectors.
All inputs are finite; a program needn't handle non-finite values.
Results may differ from the reference program's by a relative error of at most 0.02.
Values may be sent and summed in bfloat16 or wider, within the bound.
A program may use at most 64 MiB of HBM per device.

```python
import math
import jax
import jax.numpy as jnp
from jax import lax

GRID = 128
SEG = 64
C = 12
O = 16
Z = 16


def levels(stream_key, extent, pieces, low, top_value):
    level = 1.0
    for axis_at, parts in pieces:
        steps = jax.random.uniform(jax.random.fold_in(jax.random.fold_in(stream_key, 6), axis_at), (parts,), jnp.float32, low / len(pieces), top_value / len(pieces))
        level = level * jnp.repeat(jnp.exp(steps), extent[axis_at] // parts).reshape((-1,) + (1,) * (len(extent) - 1 - axis_at))
    return level


def scatter_about(own_key, extent, deviation, bound, cuts=(), kind=jnp.bfloat16):
    entries = deviation * jax.random.normal(own_key, extent, jnp.float32)
    if cuts:
        entries = entries * levels(own_key, extent, cuts, -0.22, 0.18)
    return jnp.clip(entries, -bound, bound).astype(kind)


def setup_inputs(seed: int = 0) -> dict:
    streams_of = jax.random.split(jax.random.key(seed), 7)
    return {
        "volume": scatter_about(streams_of[0], (Z, C, GRID, GRID), 1.0, 6.0, ((0, 16), (1, 2))),
        "measured": scatter_about(streams_of[1], (O, Z, SEG, GRID), 1.0, 6.0, ((0, 16),), jnp.float32),
        "basis_table": scatter_about(streams_of[2], (O, SEG, C), C ** -0.5, 1.75, ((2, 2),), jnp.float32),
        "angle_table": jnp.clip(jax.random.uniform(streams_of[3], (O,), jnp.float32, -1.2, 1.2), -1.2, 1.2),
        "angle_index": jax.random.permutation(streams_of[4], O).astype(jnp.int32),
        "sector_map": jax.vmap(lambda own: jax.random.permutation(own, SEG))(jax.random.split(streams_of[5], O)).reshape((O, SEG)).astype(jnp.int32),
    }


def dft_tables(grid_size):
    midpoint = grid_size // 2
    row_ids = jnp.arange(grid_size, dtype=jnp.int32)
    frequency = jnp.where(row_ids <= midpoint, row_ids, row_ids - midpoint)
    positions = jnp.arange(grid_size, dtype=jnp.int32)
    products = frequency[:, None] * positions[None, :] % grid_size
    radians = products.astype(jnp.float32) * (2.0 * math.pi / grid_size)
    base_wave = jnp.where((row_ids > midpoint)[:, None], jnp.sin(radians), jnp.cos(radians))
    weights = jnp.where((row_ids == 0) | (row_ids == midpoint), 1.0 / grid_size, 2.0 / grid_size).astype(jnp.float32)
    return (base_wave.astype(jnp.bfloat16), (base_wave * weights[:, None]).astype(jnp.bfloat16))

def rotate(spectrum, shifts, axis_pos):
    length = spectrum.shape[axis_pos]
    midpoint = length // 2
    row_ids = jnp.arange(length, dtype=jnp.int32)
    frequency = jnp.where(row_ids <= midpoint, row_ids, row_ids - midpoint).astype(jnp.float32)
    sign_row = jnp.where((row_ids > 0) & (row_ids < midpoint), -1.0, jnp.where(row_ids > midpoint, 1.0, 0.0)).astype(jnp.float32)
    if axis_pos == -2:
        frequency = frequency[:, None]
        sign_row = sign_row[:, None]
    phases = shifts * frequency * (2.0 * math.pi / length)
    partner = jnp.roll(spectrum, midpoint, axis=axis_pos)
    return spectrum * jnp.cos(phases) + partner * (sign_row * jnp.sin(phases))

def product(pattern, left_side, right_side):
    return jnp.einsum(pattern, left_side.astype(jnp.float32), right_side.astype(jnp.float32), precision=lax.Precision.HIGHEST)

def shifts_for(angles, grid_size):
    positions = jnp.arange(grid_size, dtype=jnp.float32) - grid_size // 2
    slope_rows = -jnp.tan(angles * 0.5)
    slope_cols = jnp.sin(angles)
    row_shift = slope_rows[:, None, None, None] * positions[None, None, :, None]
    col_shift = slope_cols[:, None, None, None] * positions[None, None, None, :]
    return (row_shift, col_shift)

def forward_items(planes, angles, mixing, analysis, synthesis):
    grid_size = planes.shape[-1]
    row_shift, col_shift = shifts_for(angles, grid_size)
    spectrum = product('kcyx,qx->kcyq', planes, analysis)
    plane_field = product('kcyq,qx->kcyx', rotate(spectrum, row_shift, -1).astype(jnp.bfloat16), synthesis).astype(jnp.bfloat16)
    spectrum = product('qy,kcyx->kcqx', analysis, plane_field)
    plane_field = product('qn,kcqx->kcnx', synthesis, rotate(spectrum, col_shift, -2).astype(jnp.bfloat16)).astype(jnp.bfloat16)
    spectrum = product('kcyx,qx->kcyq', plane_field, analysis)
    summed = lax.optimization_barrier(jnp.sum(rotate(spectrum, row_shift, -1), axis=2)).astype(jnp.bfloat16)
    profile = product('kcq,qx->kcx', summed, synthesis) * (1.0 / math.sqrt(grid_size))
    return product('ksc,kcx->ksx', mixing, profile)

def backward_items(row_block, angles, analysis, synthesis):
    grid_size = row_block.shape[-1]
    row_shift, col_shift = shifts_for(angles, grid_size)
    spectrum = product('kcx,qx->kcq', row_block, synthesis)[:, :, None, :]
    spread = (rotate(spectrum, -row_shift, -1) * (1.0 / math.sqrt(grid_size))).astype(jnp.bfloat16)
    plane_field = product('kcyq,qx->kcyx', spread, analysis).astype(jnp.bfloat16)
    spectrum = product('qn,kcnx->kcqx', synthesis, plane_field)
    plane_field = product('qn,kcqx->kcnx', analysis, rotate(spectrum, -col_shift, -2).astype(jnp.bfloat16)).astype(jnp.bfloat16)
    spectrum = product('kcyx,qx->kcyq', plane_field, synthesis)
    return product('kcyq,qx->kcyx', rotate(spectrum, -row_shift, -1).astype(jnp.bfloat16), analysis)

def reference(volume, measured, basis_table, angle_table, angle_index, sector_map):
    grid_size = volume.shape[-1]
    plane_count = volume.shape[0]
    analysis, synthesis = dft_tables(grid_size)

    def per_orient(accumulated, inputs):
        orient_index, mapping, data_rows = inputs
        angle_value = angle_table[orient_index]
        mixing_one = basis_table[orient_index][mapping]
        angles = jnp.full((plane_count,), angle_value, dtype=jnp.float32)
        mixes = jnp.broadcast_to(mixing_one[None], (plane_count,) + mixing_one.shape)
        signals = forward_items(volume, angles, mixes, analysis, synthesis)
        residual_rows = signals - data_rows
        contracted = product('zsx,zsc->zcx', residual_rows, mixes).astype(jnp.bfloat16)
        return (accumulated + backward_items(contracted, angles, analysis, synthesis), residual_rows)
    initial = jnp.zeros(volume.shape, jnp.float32)
    gradient, residual = lax.scan(per_orient, initial, (angle_index, sector_map, measured))
    return (gradient, residual)
```

```python
import functools
import math

import jax
import jax.numpy as jnp
from jax import lax
from jax.experimental import pallas as pl
from jax.experimental.pallas import tpu as pltpu
from jax.sharding import PartitionSpec as P

WIDE = jnp.float32
NARROW = jnp.bfloat16


def dft_tables(grid_size):
    midpoint = grid_size // 2
    row_ids = jnp.arange(grid_size, dtype=jnp.int32)
    frequency = jnp.where(row_ids <= midpoint, row_ids, row_ids - midpoint)
    positions = jnp.arange(grid_size, dtype=jnp.int32)
    products = frequency[:, None] * positions[None, :] % grid_size
    radians = products.astype(jnp.float32) * (2.0 * math.pi / grid_size)
    base_wave = jnp.where((row_ids > midpoint)[:, None], jnp.sin(radians), jnp.cos(radians))
    weights = jnp.where(
        (row_ids == 0) | (row_ids == midpoint), 1.0 / grid_size, 2.0 / grid_size
    ).astype(jnp.float32)
    return (base_wave.astype(jnp.bfloat16), (base_wave * weights[:, None]).astype(jnp.bfloat16))


def cmul(left, right):
    return (
        left[0] * right[0] - left[1] * right[1],
        left[0] * right[1] + left[1] * right[0],
    )


def power_rows(base, bits, rows, lanes):
    ids = lax.broadcasted_iota(jnp.int32, (rows, lanes), 0)
    result = None
    for bit in range(bits):
        on = (ids // (1 << bit)) % 2 == 1
        term = (jnp.where(on, base[0], 1.0), jnp.where(on, base[1], 0.0))
        result = term if result is None else cmul(result, term)
        base = cmul(base, base)
    return result, base


def unit_waves(angles, grid_size, unit_ref):
    half = grid_size // 2
    count = angles.shape[0]
    lanes = lax.broadcasted_iota(jnp.int32, (count, grid_size), 1)
    frequency = jnp.where(lanes <= half, lanes, lanes - half).astype(WIDE)
    unit = 2.0 * math.pi / grid_size
    slope_rows = -jnp.sin(angles * 0.5) / jnp.cos(angles * 0.5)
    row_phase = slope_rows * frequency * unit
    col_phase = jnp.sin(angles) * (lanes - half).astype(WIDE) * unit
    unit_ref[0] = jnp.cos(row_phase)
    unit_ref[1] = jnp.sin(row_phase)
    unit_ref[2] = jnp.cos(col_phase)
    unit_ref[3] = jnp.sin(col_phase)


def build_tables(which, grid_size, unit_ref, row_ref, col_ref, mix_ref, slot, synthesis):
    half = grid_size // 2
    lanes = lax.broadcasted_iota(jnp.int32, (8, grid_size), 1)
    sign = jnp.where(lanes > half, 1.0, jnp.where((lanes > 0) & (lanes < half), -1.0, 0.0))
    coarse_count = grid_size // 8
    bits = coarse_count.bit_length() - 1

    def take(at):
        return unit_ref[at, pl.ds(which, 1), :]

    fine, eighth = power_rows((take(0), take(1)), 3, 8, grid_size)
    coarse, top = power_rows(eighth, bits, coarse_count, grid_size)
    middle = (coarse[0][half // 8 : half // 8 + 1], coarse[1][half // 8 : half // 8 + 1])
    coarse = cmul(coarse, (middle[0], -middle[1]))
    for j in range(coarse_count):
        wave = cmul((coarse[0][j : j + 1], coarse[1][j : j + 1]), fine)
        row_ref[slot, 0, 8 * j : 8 * j + 8, :] = wave[0]
        row_ref[slot, 1, 8 * j : 8 * j + 8, :] = wave[1] * sign
    for part in range(2):
        mix_ref[slot, part] = jnp.dot(
            synthesis, row_ref[slot, part].astype(NARROW), preferred_element_type=WIDE
        )
    fine, eighth = power_rows((take(2), take(3)), 3, 8, grid_size)
    coarse, highest = power_rows(eighth, bits - 1, coarse_count // 2, grid_size)
    first = lax.broadcasted_iota(jnp.int32, (8, grid_size), 0) == 0
    for j in range(coarse_count // 2):
        wave = cmul((coarse[0][j : j + 1], coarse[1][j : j + 1]), fine)
        col_ref[slot, 0, 8 * j : 8 * j + 8, :] = wave[0]
        col_ref[slot, 1, 8 * j : 8 * j + 8, :] = -wave[1]
        low = wave[0] if j else jnp.where(first, highest[0], wave[0])
        col_ref[slot, 0, half + 8 * j : half + 8 * j + 8, :] = low
        col_ref[slot, 1, half + 8 * j : half + 8 * j + 8, :] = wave[1]


def swap_rows(field):
    half = field.shape[0] // 2
    return jnp.concatenate([field[half:], field[:half]], axis=0)


def mul(left, right):
    return jnp.dot(left, right, preferred_element_type=WIDE)


def image_groups(count, width=2):
    return [range(at, min(at + width, count)) for at in range(0, count, width)]


def volume_spectra(volume_ref, analysis_t, spec_ref, images, grid_size):
    for image in range(images):
        spectrum = mul(volume_ref[image], analysis_t)
        spec_ref[0, image] = spectrum
        spec_ref[1, image] = pltpu.roll(spectrum, grid_size // 2, 1)


def forward_one(slot, images, grid_size, spec_ref, row_ref, col_ref, mix_ref, waves):
    analysis, analysis_t, synthesis = waves
    sums, rolled = [], []
    for group in image_groups(images):
        fields = []
        for image in group:
            turned = spec_ref[0, image] * row_ref[slot, 0] + spec_ref[1, image] * row_ref[slot, 1]
            fields.append(mul(turned.astype(NARROW), synthesis).astype(NARROW))
        spectrum = mul(analysis, jnp.concatenate(fields, axis=1))
        for at in range(len(group)):
            own = spectrum[:, at * grid_size : (at + 1) * grid_size]
            turned = own * col_ref[slot, 0] + swap_rows(own) * col_ref[slot, 1]
            last = mul(turned.astype(NARROW), analysis_t)
            sums.append(jnp.sum(last * mix_ref[slot, 0], axis=0, keepdims=True))
            rolled.append(jnp.sum(last * mix_ref[slot, 1], axis=0, keepdims=True))
    total = jnp.concatenate(sums, axis=0)
    crossed = pltpu.roll(jnp.concatenate(rolled, axis=0), grid_size // 2, 1)
    summed = (total - crossed).astype(NARROW)
    return mul(summed, synthesis) * (1.0 / math.sqrt(grid_size))


def backward_one(slot, rows, grid_size, total_ref, row_ref, col_ref, mix_ref, waves):
    analysis, analysis_t, synthesis_t = waves
    images = rows.shape[0]
    spectra = mul(rows, synthesis_t) * (1.0 / math.sqrt(grid_size))
    crossed = pltpu.roll(spectra, grid_size // 2, 1)
    for group in image_groups(images):
        fields = []
        for image in group:
            spread = (
                spectra[image : image + 1] * mix_ref[slot, 0]
                - crossed[image : image + 1] * mix_ref[slot, 1]
            )
            own = mul(spread.astype(NARROW), analysis)
            turned = own * col_ref[slot, 0] - swap_rows(own) * col_ref[slot, 1]
            fields.append(turned.astype(NARROW))
        field = mul(analysis_t, jnp.concatenate(fields, axis=1)).astype(NARROW)
        for at, image in enumerate(group):
            own = mul(field[:, at * grid_size : (at + 1) * grid_size], synthesis_t)
            total_ref[image] += (
                own * row_ref[slot, 0]
                - pltpu.roll(own, grid_size // 2, 1) * row_ref[slot, 1]
            )


def forward_kernel(
    volume_ref, angle_ref, ana_ref, ana_t_ref, syn_ref, out_ref, unit_ref, spec_ref, row_ref, col_ref, mix_ref
):
    images, grid_size = volume_ref.shape[0], volume_ref.shape[-1]
    unit_waves(angle_ref[...], grid_size, unit_ref)
    volume_spectra(volume_ref, ana_t_ref[...], spec_ref, images, grid_size)

    def step(which, carry):
        build_tables(which, grid_size, unit_ref, row_ref, col_ref, mix_ref, 0, syn_ref[...])
        waves = (ana_ref[...], ana_t_ref[...], syn_ref[...])
        out_ref[which] = forward_one(0, images, grid_size, spec_ref, row_ref, col_ref, mix_ref, waves)
        return carry

    lax.fori_loop(0, out_ref.shape[0], step, 0)


def backward_kernel(
    rows_ref, angle_ref, ana_ref, ana_t_ref, syn_ref, syn_t_ref, out_ref, unit_ref, total_ref, row_ref, col_ref, mix_ref
):
    images, grid_size = out_ref.shape[0], out_ref.shape[-1]
    unit_waves(angle_ref[...], grid_size, unit_ref)
    total_ref[...] = jnp.zeros_like(total_ref)

    def step(which, carry):
        build_tables(which, grid_size, unit_ref, row_ref, col_ref, mix_ref, 0, syn_ref[...])
        waves = (ana_ref[...], ana_t_ref[...], syn_t_ref[...])
        backward_one(
            0, rows_ref[which].astype(NARROW), grid_size, total_ref, row_ref, col_ref, mix_ref, waves
        )
        return carry

    lax.fori_loop(0, rows_ref.shape[0], step, 0)
    for image in range(images):
        out_ref[image] = mul(total_ref[image].astype(NARROW), ana_ref[...])


VMEM = functools.partial(pl.BlockSpec, memory_space=pltpu.VMEM)
LIMIT = 40 << 20


def table_scratch(count, grid_size, slots):
    return [
        pltpu.VMEM((4, count, grid_size), WIDE),
        pltpu.VMEM((slots, 2, grid_size, grid_size), WIDE),
        pltpu.VMEM((slots, 2, grid_size, grid_size), WIDE),
        pltpu.VMEM((slots, 2, grid_size, grid_size), WIDE),
    ]


def exact(pattern, left, right):
    return jnp.einsum(pattern, left, right, precision=lax.Precision.HIGHEST)


def body(volume, measured, basis_table, angle_table, angle_index, sector_map):
    grid_size = volume.shape[-1]
    images = volume.shape[0] * volume.shape[1]
    own_coefs = basis_table.shape[2]
    table_count = angle_table.shape[0]
    seg_count = measured.shape[2]
    seg_share = seg_count // lax.axis_size("coef")
    analysis, synthesis = dft_tables(grid_size)
    angles = jnp.broadcast_to(angle_table[:, None], (table_count, grid_size))
    unit_s, row_s, col_s, mix_s = table_scratch(table_count, grid_size, 1)

    table_ids = jnp.arange(table_count, dtype=jnp.int32)
    own_hot = (angle_index[0] == table_ids).astype(WIDE)
    permute = (sector_map[0][:, None] == jnp.arange(seg_count, dtype=jnp.int32)).astype(WIDE)
    own_mix = exact("st,tc->sc", permute, exact("a,asc->sc", own_hot, basis_table))
    pulled = exact("zsx,sc->zcx", measured[0], own_mix)
    tagged = jnp.concatenate(
        [pulled, jnp.broadcast_to(angle_index[0].astype(WIDE), (pulled.shape[0], 1, grid_size))],
        axis=1,
    )
    arrived = lax.all_to_all(tagged, "orient", split_axis=0, concat_axis=0, tiled=True)
    basis_full = lax.all_gather(basis_table, "coef", axis=2, tiled=True)

    profiles = pl.pallas_call(
        forward_kernel,
        out_shape=jax.ShapeDtypeStruct((table_count, images, grid_size), WIDE),
        in_specs=[VMEM()] * 5,
        out_specs=VMEM(),
        scratch_shapes=[unit_s, pltpu.VMEM((2, images, grid_size, grid_size), WIDE), row_s, col_s, mix_s],
        compiler_params=pltpu.CompilerParams(vmem_limit_bytes=LIMIT),
    )(volume.reshape(images, grid_size, grid_size), angles, analysis, analysis.T, synthesis)

    all_profiles = lax.all_gather(profiles, "coef", axis=1, tiled=True)
    hot = (arrived[:, own_coefs, 0].astype(jnp.int32)[:, None] == table_ids).astype(WIDE)
    gram = exact("asc,asd->acd", basis_table, basis_full)
    contracted = exact("acd,adx->acx", gram, all_profiles) - exact(
        "oa,ocx->acx", hot, arrived[:, :own_coefs]
    )
    gradient = pl.pallas_call(
        backward_kernel,
        out_shape=jax.ShapeDtypeStruct((images, grid_size, grid_size), WIDE),
        in_specs=[VMEM()] * 6,
        out_specs=VMEM(),
        scratch_shapes=[unit_s, pltpu.VMEM((images, grid_size, grid_size), WIDE), row_s, col_s, mix_s],
        compiler_params=pltpu.CompilerParams(vmem_limit_bytes=LIMIT),
    )(contracted, angles, analysis, analysis.T, synthesis, synthesis.T)

    returned = lax.all_to_all(
        exact("oa,acx->ocx", hot, all_profiles), "orient", split_axis=0, concat_axis=0, tiled=True
    )
    full_mix = exact("st,tc->sc", permute, exact("a,asc->sc", own_hot, basis_full))
    start_seg = lax.axis_index("coef") * seg_share
    share_mix = lax.dynamic_slice_in_dim(full_mix, start_seg, seg_share, 0)
    share_data = lax.dynamic_slice_in_dim(measured[0], start_seg, seg_share, 1)
    residual = exact("sc,zcx->zsx", share_mix, returned) - share_data
    return (gradient.reshape(volume.shape), residual[None])


def solution(mesh):
    placed = (
        P("orient", "coef", None, None),
        P("orient", None, None, None),
        P(None, None, "coef"),
        P(),
        P("orient"),
        P("orient", None),
    )
    return jax.shard_map(
        body,
        mesh=mesh,
        in_specs=placed,
        out_specs=(P("orient", "coef", None, None), P("orient", None, "coef", None)),
        check_vma=False,
    )
```

```python
import functools
import math

import jax
import jax.numpy as jnp
from jax import lax
from jax.experimental import pallas as pl
from jax.experimental.pallas import tpu as pltpu
from jax.sharding import PartitionSpec as P

WIDE = jnp.float32
NARROW = jnp.bfloat16


def dft_tables(grid_size):
    midpoint = grid_size // 2
    row_ids = jnp.arange(grid_size, dtype=jnp.int32)
    frequency = jnp.where(row_ids <= midpoint, row_ids, row_ids - midpoint)
    positions = jnp.arange(grid_size, dtype=jnp.int32)
    products = frequency[:, None] * positions[None, :] % grid_size
    radians = products.astype(jnp.float32) * (2.0 * math.pi / grid_size)
    base_wave = jnp.where((row_ids > midpoint)[:, None], jnp.sin(radians), jnp.cos(radians))
    weights = jnp.where(
        (row_ids == 0) | (row_ids == midpoint), 1.0 / grid_size, 2.0 / grid_size
    ).astype(jnp.float32)
    return (base_wave.astype(jnp.bfloat16), (base_wave * weights[:, None]).astype(jnp.bfloat16))


def cmul(left, right):
    return (
        left[0] * right[0] - left[1] * right[1],
        left[0] * right[1] + left[1] * right[0],
    )


def power_rows(base, bits, rows, lanes):
    ids = lax.broadcasted_iota(jnp.int32, (rows, lanes), 0)
    result = None
    for bit in range(bits):
        on = (ids // (1 << bit)) % 2 == 1
        term = (jnp.where(on, base[0], 1.0), jnp.where(on, base[1], 0.0))
        result = term if result is None else cmul(result, term)
        base = cmul(base, base)
    return result, base


def unit_waves(angles, grid_size, unit_ref):
    half = grid_size // 2
    count = angles.shape[0]
    lanes = lax.broadcasted_iota(jnp.int32, (count, grid_size), 1)
    frequency = jnp.where(lanes <= half, lanes, lanes - half).astype(WIDE)
    unit = 2.0 * math.pi / grid_size
    slope_rows = -jnp.sin(angles * 0.5) / jnp.cos(angles * 0.5)
    row_phase = slope_rows * frequency * unit
    col_phase = jnp.sin(angles) * (lanes - half).astype(WIDE) * unit
    unit_ref[0] = jnp.cos(row_phase)
    unit_ref[1] = jnp.sin(row_phase)
    unit_ref[2] = jnp.cos(col_phase)
    unit_ref[3] = jnp.sin(col_phase)


def build_tables(which, grid_size, unit_ref, row_ref, col_ref, mix_ref, slot, synthesis):
    half = grid_size // 2
    lanes = lax.broadcasted_iota(jnp.int32, (8, grid_size), 1)
    sign = jnp.where(lanes > half, 1.0, jnp.where((lanes > 0) & (lanes < half), -1.0, 0.0))
    coarse_count = grid_size // 8
    bits = coarse_count.bit_length() - 1

    def take(at):
        return unit_ref[at, pl.ds(which, 1), :]

    fine, eighth = power_rows((take(0), take(1)), 3, 8, grid_size)
    coarse, top = power_rows(eighth, bits, coarse_count, grid_size)
    middle = (coarse[0][half // 8 : half // 8 + 1], coarse[1][half // 8 : half // 8 + 1])
    coarse = cmul(coarse, (middle[0], -middle[1]))
    for j in range(coarse_count):
        wave = cmul((coarse[0][j : j + 1], coarse[1][j : j + 1]), fine)
        row_ref[slot, 0, 8 * j : 8 * j + 8, :] = wave[0]
        row_ref[slot, 1, 8 * j : 8 * j + 8, :] = wave[1] * sign
    for part in range(2):
        mix_ref[slot, part] = jnp.dot(
            synthesis, row_ref[slot, part].astype(NARROW), preferred_element_type=WIDE
        )
    fine, eighth = power_rows((take(2), take(3)), 3, 8, grid_size)
    coarse, highest = power_rows(eighth, bits - 1, coarse_count // 2, grid_size)
    first = lax.broadcasted_iota(jnp.int32, (8, grid_size), 0) == 0
    for j in range(coarse_count // 2):
        wave = cmul((coarse[0][j : j + 1], coarse[1][j : j + 1]), fine)
        col_ref[slot, 0, 8 * j : 8 * j + 8, :] = wave[0]
        col_ref[slot, 1, 8 * j : 8 * j + 8, :] = -wave[1]
        low = wave[0] if j else jnp.where(first, highest[0], wave[0])
        col_ref[slot, 0, half + 8 * j : half + 8 * j + 8, :] = low
        col_ref[slot, 1, half + 8 * j : half + 8 * j + 8, :] = wave[1]


def swap_rows(field):
    half = field.shape[0] // 2
    return jnp.concatenate([field[half:], field[:half]], axis=0)


def mul(left, right):
    return jnp.dot(left, right, preferred_element_type=WIDE)


def image_groups(count, width=2):
    return [range(at, min(at + width, count)) for at in range(0, count, width)]


def volume_spectra(volume_ref, analysis_t, spec_ref, images, grid_size):
    for image in range(images):
        spectrum = mul(volume_ref[image], analysis_t)
        spec_ref[0, image] = spectrum
        spec_ref[1, image] = pltpu.roll(spectrum, grid_size // 2, 1)


def forward_one(slot, images, grid_size, spec_ref, row_ref, col_ref, mix_ref, waves):
    analysis, analysis_t, synthesis = waves
    sums, rolled = [], []
    for group in image_groups(images):
        fields = []
        for image in group:
            turned = spec_ref[0, image] * row_ref[slot, 0] + spec_ref[1, image] * row_ref[slot, 1]
            fields.append(mul(turned.astype(NARROW), synthesis).astype(NARROW))
        spectrum = mul(analysis, jnp.concatenate(fields, axis=1))
        for at in range(len(group)):
            own = spectrum[:, at * grid_size : (at + 1) * grid_size]
            turned = own * col_ref[slot, 0] + swap_rows(own) * col_ref[slot, 1]
            last = mul(turned.astype(NARROW), analysis_t)
            sums.append(jnp.sum(last * mix_ref[slot, 0], axis=0, keepdims=True))
            rolled.append(jnp.sum(last * mix_ref[slot, 1], axis=0, keepdims=True))
    total = jnp.concatenate(sums, axis=0)
    crossed = pltpu.roll(jnp.concatenate(rolled, axis=0), grid_size // 2, 1)
    summed = (total - crossed).astype(NARROW)
    return mul(summed, synthesis) * (1.0 / math.sqrt(grid_size))


def backward_one(slot, rows, grid_size, total_ref, row_ref, col_ref, mix_ref, waves):
    analysis, analysis_t, synthesis_t = waves
    images = rows.shape[0]
    spectra = mul(rows, synthesis_t) * (1.0 / math.sqrt(grid_size))
    crossed = pltpu.roll(spectra, grid_size // 2, 1)
    for group in image_groups(images):
        fields = []
        for image in group:
            spread = (
                spectra[image : image + 1] * mix_ref[slot, 0]
                - crossed[image : image + 1] * mix_ref[slot, 1]
            )
            own = mul(spread.astype(NARROW), analysis)
            turned = own * col_ref[slot, 0] - swap_rows(own) * col_ref[slot, 1]
            fields.append(turned.astype(NARROW))
        field = mul(analysis_t, jnp.concatenate(fields, axis=1)).astype(NARROW)
        for at, image in enumerate(group):
            own = mul(field[:, at * grid_size : (at + 1) * grid_size], synthesis_t)
            total_ref[image] += (
                own * row_ref[slot, 0]
                - pltpu.roll(own, grid_size // 2, 1) * row_ref[slot, 1]
            )


MESH = pl.DeviceIdType.MESH
LIMIT = 48 << 20


def exact(left, right, contract=((1,), (0,))):
    return lax.dot_general(
        left, right, (contract, ((), ())), precision=lax.Precision.HIGHEST, preferred_element_type=WIDE
    )


def whole_kernel(
    orients, coefs, own_coefs,
    volume_ref, data_ref, basis_ref, angle_ref, index_ref, map_ref, ana_ref, ana_t_ref, syn_ref, syn_t_ref,
    grad_ref, resid_ref,
    unit_ref, spec_ref, row_ref, col_ref, mix_ref, total_ref,
    basis_all, pull_out, pull_in, prof_all, back_out, back_in,
    basis_send, basis_recv, pull_send, pull_recv, prof_send, prof_recv, back_send, back_recv,
):
    me, mine = lax.axis_index("orient"), lax.axis_index("coef")
    images, grid_size = volume_ref.shape[0], volume_ref.shape[-1]
    tables, padded, segs = basis_ref.shape
    planes = data_ref.shape[0]
    share = resid_ref.shape[1]

    def ahead(step):
        return lax.rem(me + step, orients)

    def behind(step):
        return lax.rem(me + orients - step, orients)

    def basis_copy(step):
        return pltpu.make_async_remote_copy(
            src_ref=basis_ref, dst_ref=basis_all.at[mine],
            send_sem=basis_send.at[step - 1], recv_sem=basis_recv.at[step - 1],
            device_id=(me, lax.rem(mine + step, coefs)), device_id_type=MESH,
        )

    def prof_copy(step, which):
        return pltpu.make_async_remote_copy(
            src_ref=prof_all.at[which, mine], dst_ref=prof_all.at[which, mine],
            send_sem=prof_send.at[step - 1, which], recv_sem=prof_recv.at[step - 1, which],
            device_id=(me, lax.rem(mine + step, coefs)), device_id_type=MESH,
        )

    def pull_copy(step):
        return pltpu.make_async_remote_copy(
            src_ref=pull_out.at[ahead(step)], dst_ref=pull_in.at[me],
            send_sem=pull_send.at[step - 1], recv_sem=pull_recv.at[step - 1],
            device_id=(ahead(step), mine), device_id_type=MESH,
        )

    def back_copy(step):
        return pltpu.make_async_remote_copy(
            src_ref=back_out.at[ahead(step)], dst_ref=back_in.at[me],
            send_sem=back_send.at[step - 1], recv_sem=back_recv.at[step - 1],
            device_id=(ahead(step), mine), device_id_type=MESH,
        )

    def over_steps(action):
        def one(step, carry):
            action(step)
            return carry

        lax.fori_loop(1, orients, one, 0)

    barrier = pltpu.get_barrier_semaphore()
    over_steps(
        lambda step: pl.semaphore_signal(
            barrier, inc=1, device_id=(ahead(step), mine), device_id_type=MESH
        )
    )
    for step in range(1, coefs):
        pl.semaphore_signal(
            barrier, inc=1, device_id=(me, lax.rem(mine + step, coefs)), device_id_type=MESH
        )

    map_row = map_ref[...]
    chosen = (lax.broadcasted_iota(jnp.int32, (segs, segs), 0) == map_row).astype(WIDE)
    index = index_ref[0]
    own_mix_t = exact(basis_ref[index], chosen)
    tag_row = lax.broadcasted_iota(jnp.int32, (padded, grid_size), 0) == own_coefs
    tag = index.astype(WIDE)

    def pull_one(plane, carry):
        pull_out[plane] = jnp.where(tag_row, tag, exact(own_mix_t, data_ref[plane]))
        return carry

    lax.fori_loop(0, planes, pull_one, 0, unroll=4)
    pull_in[me] = pull_out[me]
    basis_all[mine] = basis_ref[...]
    pl.semaphore_wait(barrier, orients + coefs - 2)
    for step in range(1, coefs):
        basis_copy(step).start()
    over_steps(lambda step: pull_copy(step).start())

    unit_waves(angle_ref[...], grid_size, unit_ref)
    volume_spectra(volume_ref, ana_t_ref[...], spec_ref, images, grid_size)
    filler = jnp.zeros((padded - images, grid_size), WIDE)

    def project(which, carry):
        build_tables(which, grid_size, unit_ref, row_ref, col_ref, mix_ref, which, syn_ref[...])
        waves = (ana_ref[...], ana_t_ref[...], syn_ref[...])
        rows = forward_one(which, images, grid_size, spec_ref, row_ref, col_ref, mix_ref, waves)
        prof_all[which, mine] = jnp.concatenate([rows, filler], axis=0)
        for step in range(1, coefs):
            prof_copy(step, which).start()
        return carry

    lax.fori_loop(0, tables, project, 0)

    total_ref[...] = jnp.zeros_like(total_ref)
    for step in range(1, coefs):
        basis_copy(step).wait()
    over_steps(lambda step: pull_copy(step).wait())

    def arrived(which, carry):
        for step in range(1, coefs):
            prof_copy(step, which).wait()
        return carry

    def spread_back(which, carry):
        rows = jnp.zeros((padded, grid_size), WIDE)
        for orient in range(orients):
            block = pull_in[orient]
            tags = block[own_coefs : own_coefs + 1]
            rows = rows - jnp.where(tags == which.astype(WIDE), block, 0.0)
        for part in range(coefs):
            gram = exact(basis_ref[which], basis_all[part, which], ((1,), (1,)))
            rows = rows + exact(gram, prof_all[which, part])
        waves = (ana_ref[...], ana_t_ref[...], syn_t_ref[...])
        backward_one(
            which, rows[:images].astype(NARROW), grid_size, total_ref, row_ref, col_ref, mix_ref, waves
        )
        return carry

    early = tables // 2
    lax.fori_loop(0, early, lambda which, carry: spread_back(which, arrived(which, carry)), 0)
    lax.fori_loop(early, tables, arrived, 0)

    def return_one(orient, carry):
        tags = pull_in[orient][own_coefs : own_coefs + 1]

        def add(which, found):
            return found + jnp.where(tags[None] == which.astype(WIDE), prof_all[which], 0.0)

        back_out[orient] = lax.fori_loop(
            0, tables, add, jnp.zeros((coefs, padded, grid_size), WIDE), unroll=8
        )
        return carry

    lax.fori_loop(0, orients, return_one, 0)
    back_in[me] = back_out[me]
    over_steps(lambda step: back_copy(step).start())
    lax.fori_loop(early, tables, spread_back, 0)
    for image in range(images):
        grad_ref[image] = mul(total_ref[image].astype(NARROW), ana_ref[...])

    row_ids = lax.broadcasted_iota(jnp.int32, (share, segs), 0) + mine * share
    lane_ids = lax.broadcasted_iota(jnp.int32, (share, segs), 1)
    map_column = jnp.sum(
        jnp.where(row_ids == lane_ids, map_row.astype(WIDE), 0.0), axis=1, keepdims=True
    )
    picked = (lane_ids.astype(WIDE) == map_column).astype(WIDE)
    all_basis = jnp.concatenate([basis_all[part, index] for part in range(coefs)], axis=0)
    share_mix = exact(picked, all_basis, ((1,), (1,)))
    start = pl.multiple_of(mine * share, share)
    over_steps(lambda step: back_copy(step).wait())

    def residual_one(plane, carry):
        rows = back_in[plane].reshape(coefs * padded, grid_size)
        resid_ref[plane] = exact(share_mix, rows) - data_ref[plane, pl.ds(start, share), :]
        return carry

    lax.fori_loop(0, planes, residual_one, 0, unroll=4)


def body(volume, measured, basis_table, angle_table, angle_index, sector_map):
    grid_size = volume.shape[-1]
    images = volume.shape[0] * volume.shape[1]
    own_coefs = basis_table.shape[2]
    tables = angle_table.shape[0]
    planes, segs = measured.shape[1], measured.shape[2]
    orients, coefs = lax.axis_size("orient"), lax.axis_size("coef")
    share = segs // coefs
    padded = (own_coefs + 8) // 8 * 8
    analysis, synthesis = dft_tables(grid_size)
    angles = jnp.broadcast_to(angle_table[:, None], (tables, grid_size))
    basis = jnp.pad(basis_table.transpose(0, 2, 1), ((0, 0), (0, padded - own_coefs), (0, 0)))
    vmem = pl.BlockSpec(memory_space=pltpu.VMEM)
    smem = pl.BlockSpec(memory_space=pltpu.SMEM)
    table = pltpu.VMEM((tables, 2, grid_size, grid_size), WIDE)
    dma = pltpu.SemaphoreType.DMA
    gradient, residual = pl.pallas_call(
        functools.partial(whole_kernel, orients, coefs, own_coefs),
        out_shape=(
            jax.ShapeDtypeStruct((images, grid_size, grid_size), WIDE),
            jax.ShapeDtypeStruct((planes, share, grid_size), WIDE),
        ),
        in_specs=[vmem] * 4 + [smem] + [vmem] * 5,
        out_specs=(vmem, vmem),
        scratch_shapes=[
            pltpu.VMEM((4, tables, grid_size), WIDE),
            pltpu.VMEM((2, images, grid_size, grid_size), WIDE),
            table,
            table,
            table,
            pltpu.VMEM((images, grid_size, grid_size), WIDE),
            pltpu.VMEM((coefs, tables, padded, segs), WIDE),
            pltpu.VMEM((planes, padded, grid_size), WIDE),
            pltpu.VMEM((orients, padded, grid_size), WIDE),
            pltpu.VMEM((tables, coefs, padded, grid_size), WIDE),
            pltpu.VMEM((orients, coefs, padded, grid_size), WIDE),
            pltpu.VMEM((planes, coefs, padded, grid_size), WIDE),
            dma((coefs - 1,)),
            dma((coefs - 1,)),
            dma((orients - 1,)),
            dma((orients - 1,)),
            dma((coefs - 1, tables)),
            dma((coefs - 1, tables)),
            dma((orients - 1,)),
            dma((orients - 1,)),
        ],
        compiler_params=pltpu.CompilerParams(
            collective_id=0, has_side_effects=True, vmem_limit_bytes=LIMIT
        ),
    )(
        volume.reshape(images, grid_size, grid_size),
        measured[0],
        basis,
        angles,
        angle_index,
        sector_map,
        analysis,
        analysis.T,
        synthesis,
        synthesis.T,
    )
    return (gradient.reshape(volume.shape), residual[None])


def solution(mesh):
    placed = (
        P("orient", "coef", None, None),
        P("orient", None, None, None),
        P(None, None, "coef"),
        P(),
        P("orient"),
        P("orient", None),
    )
    return jax.shard_map(
        body,
        mesh=mesh,
        in_specs=placed,
        out_specs=(P("orient", "coef", None, None), P("orient", None, "coef", None)),
        check_vma=False,
    )
```

```python
import functools
import math

import jax
import jax.numpy as jnp
from jax import lax
from jax.experimental import pallas as pl
from jax.experimental.pallas import tpu as pltpu
from jax.sharding import PartitionSpec as P

WIDE = jnp.float32
NARROW = jnp.bfloat16


def dft_tables(grid_size):
    midpoint = grid_size // 2
    row_ids = jnp.arange(grid_size, dtype=jnp.int32)
    frequency = jnp.where(row_ids <= midpoint, row_ids, row_ids - midpoint)
    positions = jnp.arange(grid_size, dtype=jnp.int32)
    products = frequency[:, None] * positions[None, :] % grid_size
    radians = products.astype(jnp.float32) * (2.0 * math.pi / grid_size)
    base_wave = jnp.where((row_ids > midpoint)[:, None], jnp.sin(radians), jnp.cos(radians))
    weights = jnp.where(
        (row_ids == 0) | (row_ids == midpoint), 1.0 / grid_size, 2.0 / grid_size
    ).astype(jnp.float32)
    return (base_wave.astype(jnp.bfloat16), (base_wave * weights[:, None]).astype(jnp.bfloat16))


def cmul(left, right):
    return (
        left[0] * right[0] - left[1] * right[1],
        left[0] * right[1] + left[1] * right[0],
    )


def power_rows(base, bits, rows, lanes):
    ids = lax.broadcasted_iota(jnp.int32, (rows, lanes), 0)
    result = None
    for bit in range(bits):
        on = (ids // (1 << bit)) % 2 == 1
        term = (jnp.where(on, base[0], 1.0), jnp.where(on, base[1], 0.0))
        result = term if result is None else cmul(result, term)
        base = cmul(base, base)
    return result, base


def unit_waves(angles, grid_size, unit_ref):
    half = grid_size // 2
    count = angles.shape[0]
    lanes = lax.broadcasted_iota(jnp.int32, (count, grid_size), 1)
    frequency = jnp.where(lanes <= half, lanes, lanes - half).astype(WIDE)
    unit = 2.0 * math.pi / grid_size
    slope_rows = -jnp.sin(angles * 0.5) / jnp.cos(angles * 0.5)
    row_phase = slope_rows * frequency * unit
    col_phase = jnp.sin(angles) * (lanes - half).astype(WIDE) * unit
    unit_ref[0] = jnp.cos(row_phase)
    unit_ref[1] = jnp.sin(row_phase)
    unit_ref[2] = jnp.cos(col_phase)
    unit_ref[3] = jnp.sin(col_phase)


def build_tables(which, grid_size, unit_ref, row_ref, col_ref, mix_ref, slot, synthesis):
    half = grid_size // 2
    lanes = lax.broadcasted_iota(jnp.int32, (8, grid_size), 1)
    sign = jnp.where(lanes > half, 1.0, jnp.where((lanes > 0) & (lanes < half), -1.0, 0.0))
    coarse_count = grid_size // 8
    bits = coarse_count.bit_length() - 1

    def take(at):
        return unit_ref[at, pl.ds(which, 1), :]

    fine, eighth = power_rows((take(0), take(1)), 3, 8, grid_size)
    coarse, top = power_rows(eighth, bits, coarse_count, grid_size)
    middle = (coarse[0][half // 8 : half // 8 + 1], coarse[1][half // 8 : half // 8 + 1])
    coarse = cmul(coarse, (middle[0], -middle[1]))
    for j in range(coarse_count):
        wave = cmul((coarse[0][j : j + 1], coarse[1][j : j + 1]), fine)
        row_ref[slot, 0, 8 * j : 8 * j + 8, :] = wave[0]
        row_ref[slot, 1, 8 * j : 8 * j + 8, :] = wave[1] * sign
    for part in range(2):
        mix_ref[slot, part] = jnp.dot(
            synthesis, row_ref[slot, part].astype(NARROW), preferred_element_type=WIDE
        )
    fine, eighth = power_rows((take(2), take(3)), 3, 8, grid_size)
    coarse, highest = power_rows(eighth, bits - 1, coarse_count // 2, grid_size)
    first = lax.broadcasted_iota(jnp.int32, (8, grid_size), 0) == 0
    for j in range(coarse_count // 2):
        wave = cmul((coarse[0][j : j + 1], coarse[1][j : j + 1]), fine)
        col_ref[slot, 0, 8 * j : 8 * j + 8, :] = wave[0]
        col_ref[slot, 1, 8 * j : 8 * j + 8, :] = -wave[1]
        low = wave[0] if j else jnp.where(first, highest[0], wave[0])
        col_ref[slot, 0, half + 8 * j : half + 8 * j + 8, :] = low
        col_ref[slot, 1, half + 8 * j : half + 8 * j + 8, :] = wave[1]


def swap_rows(field):
    half = field.shape[0] // 2
    return jnp.concatenate([field[half:], field[:half]], axis=0)


def mul(left, right):
    return jnp.dot(left, right, preferred_element_type=WIDE)


def image_groups(count, width=2):
    return [range(at, min(at + width, count)) for at in range(0, count, width)]


def volume_spectra(volume_ref, analysis_t, spec_ref, images, grid_size):
    for image in range(images):
        spectrum = mul(volume_ref[image], analysis_t)
        spec_ref[0, image] = spectrum
        spec_ref[1, image] = pltpu.roll(spectrum, grid_size // 2, 1)


def forward_pair(slot, images, grid_size, spec_ref, sides, waves):
    analysis, analysis_t, synthesis = waves
    half = grid_size // 2
    sums, rolled = [[] for _ in sides], [[] for _ in sides]
    for group in image_groups(images):
        spectra = []
        for row_ref, _, _ in sides:
            fields = []
            for image in group:
                turned = (
                    spec_ref[0, image] * row_ref[slot, 0] + spec_ref[1, image] * row_ref[slot, 1]
                )
                fields.append(mul(turned.astype(NARROW), synthesis).astype(NARROW))
            spectra.append(mul(analysis, jnp.concatenate(fields, axis=1)))
        for side, (_, col_ref, mix_ref) in enumerate(sides):
            for at in range(len(group)):
                own = spectra[side][:, at * grid_size : (at + 1) * grid_size]
                turned = own * col_ref[slot, 0] + swap_rows(own) * col_ref[slot, 1]
                last = mul(turned.astype(NARROW), analysis_t)
                sums[side].append(jnp.sum(last * mix_ref[slot, 0], axis=0, keepdims=True))
                rolled[side].append(jnp.sum(last * mix_ref[slot, 1], axis=0, keepdims=True))
    profiles = []
    for side in range(len(sides)):
        total = jnp.concatenate(sums[side], axis=0)
        crossed = pltpu.roll(jnp.concatenate(rolled[side], axis=0), half, 1)
        summed = (total - crossed).astype(NARROW)
        profiles.append(mul(summed, synthesis) * (1.0 / math.sqrt(grid_size)))
    return profiles


def backward_pair(slot, spectra, images, grid_size, total_ref, sides, waves):
    analysis, analysis_t, synthesis_t = waves
    half = grid_size // 2
    for group in image_groups(images):
        spread_out = []
        for (own_rows, crossed), (_, col_ref, mix_ref) in zip(spectra, sides):
            fields = []
            for image in group:
                spread = (
                    own_rows[image : image + 1] * mix_ref[slot, 0]
                    - crossed[image : image + 1] * mix_ref[slot, 1]
                )
                own = mul(spread.astype(NARROW), analysis)
                turned = own * col_ref[slot, 0] - swap_rows(own) * col_ref[slot, 1]
                fields.append(turned.astype(NARROW))
            spread_out.append(mul(analysis_t, jnp.concatenate(fields, axis=1)).astype(NARROW))
        for at, image in enumerate(group):
            added = None
            for field, (row_ref, _, _) in zip(spread_out, sides):
                own = mul(field[:, at * grid_size : (at + 1) * grid_size], synthesis_t)
                turned = own * row_ref[slot, 0] - pltpu.roll(own, half, 1) * row_ref[slot, 1]
                added = turned if added is None else added + turned
            total_ref[image] += added


def split(value):
    high = value.astype(NARROW)
    return high, (value - high.astype(WIDE)).astype(NARROW)


MESH = pl.DeviceIdType.MESH
LIMIT = 48 << 20


def exact(left, right, contract=((1,), (0,))):
    return lax.dot_general(
        left, right, (contract, ((), ())), precision=lax.Precision.HIGHEST, preferred_element_type=WIDE
    )


def whole_kernel(
    orients, coefs, own_coefs,
    volume_ref, data_ref, basis_ref, angle_ref, index_ref, map_ref, ana_ref, ana_t_ref, syn_ref, syn_t_ref,
    grad_ref, resid_ref,
    unit_ref, spec_ref, row_a, col_a, mix_a, row_b, col_b, mix_b, total_ref,
    basis_all, pull_out, pull_in, prof_all, back_out, back_in,
    basis_send, basis_recv, pull_send, pull_recv, prof_send, prof_recv, back_send, back_recv,
):
    me, mine = lax.axis_index("orient"), lax.axis_index("coef")
    images, grid_size = volume_ref.shape[0], volume_ref.shape[-1]
    tables, padded, segs = basis_ref.shape
    planes = data_ref.shape[0]
    share = resid_ref.shape[1]

    def ahead(step):
        return lax.rem(me + step, orients)

    def behind(step):
        return lax.rem(me + orients - step, orients)

    def basis_copy(step):
        return pltpu.make_async_remote_copy(
            src_ref=basis_ref, dst_ref=basis_all.at[mine],
            send_sem=basis_send.at[step - 1], recv_sem=basis_recv.at[step - 1],
            device_id=(me, lax.rem(mine + step, coefs)), device_id_type=MESH,
        )

    def prof_copy(step, which):
        return pltpu.make_async_remote_copy(
            src_ref=prof_all.at[which, mine], dst_ref=prof_all.at[which, mine],
            send_sem=prof_send.at[step - 1, which], recv_sem=prof_recv.at[step - 1, which],
            device_id=(me, lax.rem(mine + step, coefs)), device_id_type=MESH,
        )

    def pull_copy(step):
        return pltpu.make_async_remote_copy(
            src_ref=pull_out.at[ahead(step)], dst_ref=pull_in.at[me],
            send_sem=pull_send.at[step - 1], recv_sem=pull_recv.at[step - 1],
            device_id=(ahead(step), mine), device_id_type=MESH,
        )

    def back_copy(step):
        return pltpu.make_async_remote_copy(
            src_ref=back_out.at[ahead(step)], dst_ref=back_in.at[me],
            send_sem=back_send.at[step - 1], recv_sem=back_recv.at[step - 1],
            device_id=(ahead(step), mine), device_id_type=MESH,
        )

    def over_steps(action):
        def one(step, carry):
            action(step)
            return carry

        lax.fori_loop(1, orients, one, 0)

    barrier = pltpu.get_barrier_semaphore()
    over_steps(
        lambda step: pl.semaphore_signal(
            barrier, inc=1, device_id=(ahead(step), mine), device_id_type=MESH
        )
    )
    for step in range(1, coefs):
        pl.semaphore_signal(
            barrier, inc=1, device_id=(me, lax.rem(mine + step, coefs)), device_id_type=MESH
        )

    unit_waves(angle_ref[...], grid_size, unit_ref)
    volume_spectra(volume_ref, ana_t_ref[...], spec_ref, images, grid_size)
    total_ref[...] = jnp.zeros_like(total_ref)
    map_row = map_ref[...]
    chosen = (lax.broadcasted_iota(jnp.int32, (segs, segs), 0) == map_row).astype(WIDE)
    index = index_ref[0]
    own_mix_t = exact(basis_ref[index], chosen)
    tag_row = lax.broadcasted_iota(jnp.int32, (padded, grid_size), 0) == own_coefs
    tag = index.astype(WIDE)

    mix_parts = jnp.concatenate(split(own_mix_t), axis=0)

    def pull_one(plane, carry):
        both = mul(mix_parts, data_ref[plane].astype(NARROW))
        pull_out[plane] = jnp.where(tag_row, tag, both[:padded] + both[padded:])
        return carry

    lax.fori_loop(0, planes, pull_one, 0, unroll=8)
    pull_in[me] = pull_out[me]
    basis_all[mine] = basis_ref[...]
    pl.semaphore_wait(barrier, orients + coefs - 2)
    for step in range(1, coefs):
        basis_copy(step).start()
    over_steps(lambda step: pull_copy(step).start())

    filler = jnp.zeros((padded - images, grid_size), WIDE)

    sides = ((row_a, col_a, mix_a), (row_b, col_b, mix_b))
    pairs = tables // 2

    def project(slot, carry):
        for side, refs in enumerate(sides):
            build_tables(2 * slot + side, grid_size, unit_ref, *refs, slot, syn_ref[...])
        waves = (ana_ref[...], ana_t_ref[...], syn_ref[...])
        profiles = forward_pair(slot, images, grid_size, spec_ref, sides, waves)
        for side, rows in enumerate(profiles):
            prof_all[2 * slot + side, mine] = jnp.concatenate([rows, filler], axis=0)
        for side in range(2):
            for step in range(1, coefs):
                prof_copy(step, 2 * slot + side).start()
        return carry

    lax.fori_loop(0, pairs, project, 0)

    for step in range(1, coefs):
        basis_copy(step).wait()
    over_steps(lambda step: pull_copy(step).wait())

    def arrived(slot, carry):
        for side in range(2):
            for step in range(1, coefs):
                prof_copy(step, 2 * slot + side).wait()
        return carry

    def contract(slot):
        found = []
        for side in range(2):
            which = 2 * slot + side
            rows = jnp.zeros((padded, grid_size), WIDE)
            for orient in range(orients):
                block = pull_in[orient]
                tags = block[own_coefs : own_coefs + 1]
                rows = rows - jnp.where(tags == lax.convert_element_type(which, WIDE), block, 0.0)
            for part in range(coefs):
                gram = exact(basis_ref[which], basis_all[part, which], ((1,), (1,)))
                rows = rows + exact(gram, prof_all[which, part])
            spectra = mul(rows.astype(NARROW), syn_t_ref[...]) * (1.0 / math.sqrt(grid_size))
            found.append((spectra, pltpu.roll(spectra, grid_size // 2, 1)))
        return tuple(found)

    def spread_back(slot, spectra):
        waves = (ana_ref[...], ana_t_ref[...], syn_t_ref[...])
        following = contract(jnp.minimum(slot + 1, pairs - 1))
        backward_pair(slot, spectra, images, grid_size, total_ref, sides, waves)
        return following

    def first_part(slot, spectra):
        arrived(slot + 1, 0)
        return spread_back(slot, spectra)

    early = pairs // 2
    arrived(0, 0)
    spectra = lax.fori_loop(0, early, first_part, contract(jnp.int32(0)))
    lax.fori_loop(early + 1, pairs, arrived, 0)

    def return_one(orient, carry):
        tags = pull_in[orient][own_coefs : own_coefs + 1]

        def add(which, found):
            return found + jnp.where(tags[None] == which.astype(WIDE), prof_all[which], 0.0)

        back_out[orient] = lax.fori_loop(
            0, tables, add, jnp.zeros((coefs, padded, grid_size), WIDE), unroll=16
        )
        return carry

    lax.fori_loop(0, orients, return_one, 0)
    back_in[me] = back_out[me]
    over_steps(lambda step: back_copy(step).start())
    lax.fori_loop(early, pairs, spread_back, spectra)
    for image in range(images):
        grad_ref[image] = mul(total_ref[image].astype(NARROW), ana_ref[...])

    row_ids = lax.broadcasted_iota(jnp.int32, (share, segs), 0) + mine * share
    lane_ids = lax.broadcasted_iota(jnp.int32, (share, segs), 1)
    map_column = jnp.sum(
        jnp.where(row_ids == lane_ids, map_row.astype(WIDE), 0.0), axis=1, keepdims=True
    )
    picked = (lane_ids.astype(WIDE) == map_column).astype(WIDE)
    all_basis = jnp.concatenate([basis_all[part, index] for part in range(coefs)], axis=0)
    high, low = split(exact(picked, all_basis, ((1,), (1,))))
    share_mix = jnp.concatenate([high, low, high], axis=1)
    start = pl.multiple_of(mine * share, share)
    over_steps(lambda step: back_copy(step).wait())

    def residual_one(plane, carry):
        rows = back_in[plane].reshape(coefs * padded, grid_size)
        high, low = split(rows)
        signals = mul(share_mix, jnp.concatenate([high, high, low], axis=0))
        resid_ref[plane] = signals - data_ref[plane, pl.ds(start, share), :]
        return carry

    lax.fori_loop(0, planes, residual_one, 0, unroll=8)


def body(volume, measured, basis_table, angle_table, angle_index, sector_map):
    grid_size = volume.shape[-1]
    images = volume.shape[0] * volume.shape[1]
    own_coefs = basis_table.shape[2]
    tables = angle_table.shape[0]
    planes, segs = measured.shape[1], measured.shape[2]
    orients, coefs = lax.axis_size("orient"), lax.axis_size("coef")
    share = segs // coefs
    padded = (own_coefs + 8) // 8 * 8
    analysis, synthesis = dft_tables(grid_size)
    angles = jnp.broadcast_to(angle_table[:, None], (tables, grid_size))
    basis = jnp.pad(basis_table.transpose(0, 2, 1), ((0, 0), (0, padded - own_coefs), (0, 0)))
    vmem = pl.BlockSpec(memory_space=pltpu.VMEM)
    smem = pl.BlockSpec(memory_space=pltpu.SMEM)
    table = pltpu.VMEM((tables // 2, 2, grid_size, grid_size), WIDE)
    dma = pltpu.SemaphoreType.DMA
    gradient, residual = pl.pallas_call(
        functools.partial(whole_kernel, orients, coefs, own_coefs),
        out_shape=(
            jax.ShapeDtypeStruct((images, grid_size, grid_size), WIDE),
            jax.ShapeDtypeStruct((planes, share, grid_size), WIDE),
        ),
        in_specs=[vmem] * 4 + [smem] + [vmem] * 5,
        out_specs=(vmem, vmem),
        scratch_shapes=[
            pltpu.VMEM((4, tables, grid_size), WIDE),
            pltpu.VMEM((2, images, grid_size, grid_size), WIDE),
            *[table] * 6,
            pltpu.VMEM((images, grid_size, grid_size), WIDE),
            pltpu.VMEM((coefs, tables, padded, segs), WIDE),
            pltpu.VMEM((planes, padded, grid_size), WIDE),
            pltpu.VMEM((orients, padded, grid_size), WIDE),
            pltpu.VMEM((tables, coefs, padded, grid_size), WIDE),
            pltpu.VMEM((orients, coefs, padded, grid_size), WIDE),
            pltpu.VMEM((planes, coefs, padded, grid_size), WIDE),
            dma((coefs - 1,)),
            dma((coefs - 1,)),
            dma((orients - 1,)),
            dma((orients - 1,)),
            dma((coefs - 1, tables)),
            dma((coefs - 1, tables)),
            dma((orients - 1,)),
            dma((orients - 1,)),
        ],
        compiler_params=pltpu.CompilerParams(
            collective_id=0, has_side_effects=True, vmem_limit_bytes=LIMIT
        ),
    )(
        volume.reshape(images, grid_size, grid_size),
        measured[0],
        basis,
        angles,
        angle_index,
        sector_map,
        analysis,
        analysis.T,
        synthesis,
        synthesis.T,
    )
    return (gradient.reshape(volume.shape), residual[None])


def solution(mesh):
    placed = (
        P("orient", "coef", None, None),
        P("orient", None, None, None),
        P(None, None, "coef"),
        P(),
        P("orient"),
        P("orient", None),
    )
    return jax.shard_map(
        body,
        mesh=mesh,
        in_specs=placed,
        out_specs=(P("orient", "coef", None, None), P("orient", None, "coef", None)),
        check_vma=False,
    )
```

```python
import functools
import math

import jax
import jax.numpy as jnp
from jax import lax
from jax.experimental import pallas as pl
from jax.experimental.pallas import tpu as pltpu
from jax.sharding import PartitionSpec as P

WIDE = jnp.float32
NARROW = jnp.bfloat16


def dft_tables(grid_size):
    midpoint = grid_size // 2
    row_ids = jnp.arange(grid_size, dtype=jnp.int32)
    frequency = jnp.where(row_ids <= midpoint, row_ids, row_ids - midpoint)
    positions = jnp.arange(grid_size, dtype=jnp.int32)
    products = frequency[:, None] * positions[None, :] % grid_size
    radians = products.astype(jnp.float32) * (2.0 * math.pi / grid_size)
    base_wave = jnp.where((row_ids > midpoint)[:, None], jnp.sin(radians), jnp.cos(radians))
    weights = jnp.where(
        (row_ids == 0) | (row_ids == midpoint), 1.0 / grid_size, 2.0 / grid_size
    ).astype(jnp.float32)
    return (base_wave.astype(jnp.bfloat16), (base_wave * weights[:, None]).astype(jnp.bfloat16))


def cmul(left, right):
    return (
        left[0] * right[0] - left[1] * right[1],
        left[0] * right[1] + left[1] * right[0],
    )


def power_rows(base, bits, rows, lanes):
    ids = lax.broadcasted_iota(jnp.int32, (rows, lanes), 0)
    result = None
    for bit in range(bits):
        on = (ids // (1 << bit)) % 2 == 1
        term = (jnp.where(on, base[0], 1.0), jnp.where(on, base[1], 0.0))
        result = term if result is None else cmul(result, term)
        base = cmul(base, base)
    return result, base


def unit_waves(angles, grid_size, unit_ref):
    half = grid_size // 2
    count = angles.shape[0]
    lanes = lax.broadcasted_iota(jnp.int32, (count, grid_size), 1)
    frequency = jnp.where(lanes <= half, lanes, lanes - half).astype(WIDE)
    unit = 2.0 * math.pi / grid_size
    slope_rows = -jnp.sin(angles * 0.5) / jnp.cos(angles * 0.5)
    row_phase = slope_rows * frequency * unit
    col_phase = jnp.sin(angles) * (lanes - half).astype(WIDE) * unit
    unit_ref[0] = jnp.cos(row_phase)
    unit_ref[1] = jnp.sin(row_phase)
    unit_ref[2] = jnp.cos(col_phase)
    unit_ref[3] = jnp.sin(col_phase)


def build_tables(which, grid_size, unit_ref, row_ref, col_ref, mix_ref, slot, synthesis):
    half = grid_size // 2
    lanes = lax.broadcasted_iota(jnp.int32, (8, grid_size), 1)
    sign = jnp.where(lanes > half, 1.0, jnp.where((lanes > 0) & (lanes < half), -1.0, 0.0))
    coarse_count = grid_size // 8
    bits = coarse_count.bit_length() - 1

    def take(at):
        return unit_ref[at, pl.ds(which, 1), :]

    fine, eighth = power_rows((take(0), take(1)), 3, 8, grid_size)
    coarse, top = power_rows(eighth, bits, coarse_count, grid_size)
    middle = (coarse[0][half // 8 : half // 8 + 1], coarse[1][half // 8 : half // 8 + 1])
    coarse = cmul(coarse, (middle[0], -middle[1]))
    for j in range(coarse_count):
        wave = cmul((coarse[0][j : j + 1], coarse[1][j : j + 1]), fine)
        row_ref[slot, 0, 8 * j : 8 * j + 8, :] = wave[0]
        row_ref[slot, 1, 8 * j : 8 * j + 8, :] = wave[1] * sign
    for part in range(2):
        mix_ref[slot, part] = jnp.dot(
            synthesis, row_ref[slot, part].astype(NARROW), preferred_element_type=WIDE
        )
    fine, eighth = power_rows((take(2), take(3)), 3, 8, grid_size)
    coarse, highest = power_rows(eighth, bits - 1, coarse_count // 2, grid_size)
    first = lax.broadcasted_iota(jnp.int32, (8, grid_size), 0) == 0
    for j in range(coarse_count // 2):
        wave = cmul((coarse[0][j : j + 1], coarse[1][j : j + 1]), fine)
        col_ref[slot, 0, 8 * j : 8 * j + 8, :] = wave[0]
        col_ref[slot, 1, 8 * j : 8 * j + 8, :] = -wave[1]
        low = wave[0] if j else jnp.where(first, highest[0], wave[0])
        col_ref[slot, 0, half + 8 * j : half + 8 * j + 8, :] = low
        col_ref[slot, 1, half + 8 * j : half + 8 * j + 8, :] = wave[1]


def swap_rows(field):
    half = field.shape[0] // 2
    return jnp.concatenate([field[half:], field[:half]], axis=0)


def mul(left, right):
    return jnp.dot(left, right, preferred_element_type=WIDE)


def image_groups(count, width=2):
    return [range(at, min(at + width, count)) for at in range(0, count, width)]


def volume_spectra(volume_ref, analysis_t, spec_ref, images, grid_size):
    for image in range(images):
        spectrum = mul(volume_ref[image], analysis_t)
        spec_ref[0, image] = spectrum
        spec_ref[1, image] = pltpu.roll(spectrum, grid_size // 2, 1)


def forward_pair(slot, images, grid_size, spec_ref, sides, waves):
    analysis, analysis_t, synthesis = waves
    half = grid_size // 2
    sums, rolled = [[] for _ in sides], [[] for _ in sides]
    for group in image_groups(images):
        spectra = []
        for row_ref, _, _ in sides:
            fields = []
            for image in group:
                turned = (
                    spec_ref[0, image] * row_ref[slot, 0] + spec_ref[1, image] * row_ref[slot, 1]
                )
                fields.append(mul(turned.astype(NARROW), synthesis).astype(NARROW))
            spectra.append(mul(analysis, jnp.concatenate(fields, axis=1)))
        for side, (_, col_ref, mix_ref) in enumerate(sides):
            for at in range(len(group)):
                own = spectra[side][:, at * grid_size : (at + 1) * grid_size]
                turned = own * col_ref[slot, 0] + swap_rows(own) * col_ref[slot, 1]
                last = mul(turned.astype(NARROW), analysis_t)
                sums[side].append(jnp.sum(last * mix_ref[slot, 0], axis=0, keepdims=True))
                rolled[side].append(jnp.sum(last * mix_ref[slot, 1], axis=0, keepdims=True))
    profiles = []
    for side in range(len(sides)):
        total = jnp.concatenate(sums[side], axis=0)
        crossed = pltpu.roll(jnp.concatenate(rolled[side], axis=0), half, 1)
        summed = (total - crossed).astype(NARROW)
        profiles.append(mul(summed, synthesis) * (1.0 / math.sqrt(grid_size)))
    return profiles


def backward_pair(slot, spectra, images, grid_size, total_ref, sides, waves):
    analysis, analysis_t, synthesis_t = waves
    half = grid_size // 2
    for group in image_groups(images):
        spread_out = []
        for (own_rows, crossed), (_, col_ref, mix_ref) in zip(spectra, sides):
            fields = []
            for image in group:
                spread = (
                    own_rows[image : image + 1] * mix_ref[slot, 0]
                    - crossed[image : image + 1] * mix_ref[slot, 1]
                )
                own = mul(spread.astype(NARROW), analysis)
                turned = own * col_ref[slot, 0] - swap_rows(own) * col_ref[slot, 1]
                fields.append(turned.astype(NARROW))
            spread_out.append(mul(analysis_t, jnp.concatenate(fields, axis=1)).astype(NARROW))
        for at, image in enumerate(group):
            added = None
            for field, (row_ref, _, _) in zip(spread_out, sides):
                own = mul(field[:, at * grid_size : (at + 1) * grid_size], synthesis_t)
                turned = own * row_ref[slot, 0] - pltpu.roll(own, half, 1) * row_ref[slot, 1]
                added = turned if added is None else added + turned
            total_ref[image] += added


def split(value):
    high = value.astype(NARROW)
    return high, (value - high.astype(WIDE)).astype(NARROW)


MESH = pl.DeviceIdType.MESH
LIMIT = 48 << 20


def exact(left, right, contract=((1,), (0,))):
    return lax.dot_general(
        left, right, (contract, ((), ())), precision=lax.Precision.HIGHEST, preferred_element_type=WIDE
    )


def whole_kernel(
    orients, coefs, own_coefs,
    volume_ref, data_ref, basis_ref, angle_ref, index_ref, map_ref, ana_ref, ana_t_ref, syn_ref, syn_t_ref,
    grad_ref, resid_ref,
    unit_ref, spec_ref, sides, total_ref,
    basis_all, pull_out, pull_in, prof_all, back_out, back_in,
    basis_send, basis_recv, pull_send, pull_recv, prof_send, prof_recv, back_send, back_recv,
):
    me, mine = lax.axis_index("orient"), lax.axis_index("coef")
    images, grid_size = volume_ref.shape[0], volume_ref.shape[-1]
    tables, padded, segs = basis_ref.shape
    planes = data_ref.shape[0]
    share = resid_ref.shape[1]

    def ahead(step):
        return lax.rem(me + step, orients)

    def behind(step):
        return lax.rem(me + orients - step, orients)

    def basis_copy(step):
        return pltpu.make_async_remote_copy(
            src_ref=basis_ref, dst_ref=basis_all.at[mine],
            send_sem=basis_send.at[step - 1], recv_sem=basis_recv.at[step - 1],
            device_id=(me, lax.rem(mine + step, coefs)), device_id_type=MESH,
        )

    def prof_copy(step, which):
        return pltpu.make_async_remote_copy(
            src_ref=prof_all.at[which, mine], dst_ref=prof_all.at[which, mine],
            send_sem=prof_send.at[step - 1, which], recv_sem=prof_recv.at[step - 1, which],
            device_id=(me, lax.rem(mine + step, coefs)), device_id_type=MESH,
        )

    def pull_copy(step):
        return pltpu.make_async_remote_copy(
            src_ref=pull_out.at[ahead(step)], dst_ref=pull_in.at[me],
            send_sem=pull_send.at[step - 1], recv_sem=pull_recv.at[step - 1],
            device_id=(ahead(step), mine), device_id_type=MESH,
        )

    def back_copy(step):
        return pltpu.make_async_remote_copy(
            src_ref=back_out.at[ahead(step)], dst_ref=back_in.at[me],
            send_sem=back_send.at[step - 1], recv_sem=back_recv.at[step - 1],
            device_id=(ahead(step), mine), device_id_type=MESH,
        )

    def over_steps(action):
        def one(step, carry):
            action(step)
            return carry

        lax.fori_loop(1, orients, one, 0)

    barrier = pltpu.get_barrier_semaphore()
    over_steps(
        lambda step: pl.semaphore_signal(
            barrier, inc=1, device_id=(ahead(step), mine), device_id_type=MESH
        )
    )
    for step in range(1, coefs):
        pl.semaphore_signal(
            barrier, inc=1, device_id=(me, lax.rem(mine + step, coefs)), device_id_type=MESH
        )

    unit_waves(angle_ref[...], grid_size, unit_ref)
    volume_spectra(volume_ref, ana_t_ref[...], spec_ref, images, grid_size)
    total_ref[...] = jnp.zeros_like(total_ref)
    map_row = map_ref[...]
    chosen = (lax.broadcasted_iota(jnp.int32, (segs, segs), 0) == map_row).astype(WIDE)
    index = index_ref[0]
    own_mix_t = exact(basis_ref[index], chosen)
    tag_row = lax.broadcasted_iota(jnp.int32, (padded, grid_size), 0) == own_coefs
    tag = index.astype(WIDE)

    mix_parts = jnp.concatenate(split(own_mix_t), axis=0)

    def pull_one(plane, carry):
        both = mul(mix_parts, data_ref[plane].astype(NARROW))
        pull_out[plane] = jnp.where(tag_row, tag, both[:padded] + both[padded:])
        return carry

    lax.fori_loop(0, planes, pull_one, 0, unroll=8)
    pull_in[me] = pull_out[me]
    basis_all[mine] = basis_ref[...]
    pl.semaphore_wait(barrier, orients + coefs - 2)
    for step in range(1, coefs):
        basis_copy(step).start()
    over_steps(lambda step: pull_copy(step).start())

    filler = jnp.zeros((padded - images, grid_size), WIDE)

    width = len(sides)
    pairs = tables // width

    def project(slot, carry):
        for side, refs in enumerate(sides):
            build_tables(width * slot + side, grid_size, unit_ref, *refs, slot, syn_ref[...])
        waves = (ana_ref[...], ana_t_ref[...], syn_ref[...])
        profiles = forward_pair(slot, images, grid_size, spec_ref, sides, waves)
        for side, rows in enumerate(profiles):
            prof_all[width * slot + side, mine] = jnp.concatenate([rows, filler], axis=0)
        for side in range(width):
            for step in range(1, coefs):
                prof_copy(step, width * slot + side).start()
        return carry

    lax.fori_loop(0, pairs, project, 0)

    for step in range(1, coefs):
        basis_copy(step).wait()
    over_steps(lambda step: pull_copy(step).wait())

    def arrived(slot, carry):
        for side in range(width):
            for step in range(1, coefs):
                prof_copy(step, width * slot + side).wait()
        return carry

    def contract(slot):
        found = []
        for side in range(width):
            which = width * slot + side
            rows = jnp.zeros((padded, grid_size), WIDE)
            for orient in range(orients):
                block = pull_in[orient]
                tags = block[own_coefs : own_coefs + 1]
                rows = rows - jnp.where(tags == lax.convert_element_type(which, WIDE), block, 0.0)
            for part in range(coefs):
                gram = exact(basis_ref[which], basis_all[part, which], ((1,), (1,)))
                rows = rows + exact(gram, prof_all[which, part])
            spectra = mul(rows.astype(NARROW), syn_t_ref[...]) * (1.0 / math.sqrt(grid_size))
            found.append((spectra, pltpu.roll(spectra, grid_size // 2, 1)))
        return tuple(found)

    def spread_back(slot, spectra):
        waves = (ana_ref[...], ana_t_ref[...], syn_t_ref[...])
        following = contract(jnp.minimum(slot + 1, pairs - 1))
        backward_pair(slot, spectra, images, grid_size, total_ref, sides, waves)
        return following

    def first_part(slot, spectra):
        arrived(slot + 1, 0)
        return spread_back(slot, spectra)

    early = pairs // 2
    arrived(0, 0)
    spectra = lax.fori_loop(0, early, first_part, contract(jnp.int32(0)))
    lax.fori_loop(early + 1, pairs, arrived, 0)

    def return_one(orient, carry):
        tags = pull_in[orient][own_coefs : own_coefs + 1]

        def add(which, found):
            return found + jnp.where(tags[None] == which.astype(WIDE), prof_all[which], 0.0)

        back_out[orient] = lax.fori_loop(
            0, tables, add, jnp.zeros((coefs, padded, grid_size), WIDE), unroll=16
        )
        return carry

    lax.fori_loop(0, orients, return_one, 0)
    back_in[me] = back_out[me]
    over_steps(lambda step: back_copy(step).start())
    lax.fori_loop(early, pairs, spread_back, spectra)
    for image in range(images):
        grad_ref[image] = mul(total_ref[image].astype(NARROW), ana_ref[...])

    row_ids = lax.broadcasted_iota(jnp.int32, (share, segs), 0) + mine * share
    lane_ids = lax.broadcasted_iota(jnp.int32, (share, segs), 1)
    map_column = jnp.sum(
        jnp.where(row_ids == lane_ids, map_row.astype(WIDE), 0.0), axis=1, keepdims=True
    )
    picked = (lane_ids.astype(WIDE) == map_column).astype(WIDE)
    all_basis = jnp.concatenate([basis_all[part, index] for part in range(coefs)], axis=0)
    high, low = split(exact(picked, all_basis, ((1,), (1,))))
    share_mix = jnp.concatenate([high, low, high], axis=1)
    start = pl.multiple_of(mine * share, share)
    over_steps(lambda step: back_copy(step).wait())

    def residual_one(plane, carry):
        rows = back_in[plane].reshape(coefs * padded, grid_size)
        high, low = split(rows)
        signals = mul(share_mix, jnp.concatenate([high, high, low], axis=0))
        resid_ref[plane] = signals - data_ref[plane, pl.ds(start, share), :]
        return carry

    lax.fori_loop(0, planes, residual_one, 0, unroll=8)


def body(volume, measured, basis_table, angle_table, angle_index, sector_map):
    grid_size = volume.shape[-1]
    images = volume.shape[0] * volume.shape[1]
    own_coefs = basis_table.shape[2]
    tables = angle_table.shape[0]
    planes, segs = measured.shape[1], measured.shape[2]
    orients, coefs = lax.axis_size("orient"), lax.axis_size("coef")
    share = segs // coefs
    padded = (own_coefs + 8) // 8 * 8
    analysis, synthesis = dft_tables(grid_size)
    angles = jnp.broadcast_to(angle_table[:, None], (tables, grid_size))
    basis = jnp.pad(basis_table.transpose(0, 2, 1), ((0, 0), (0, padded - own_coefs), (0, 0)))
    vmem = pl.BlockSpec(memory_space=pltpu.VMEM)
    smem = pl.BlockSpec(memory_space=pltpu.SMEM)
    width = math.gcd(tables, 4)
    table = pltpu.VMEM((tables // width, 2, grid_size, grid_size), WIDE)
    dma = pltpu.SemaphoreType.DMA
    gradient, residual = pl.pallas_call(
        functools.partial(whole_kernel, orients, coefs, own_coefs),
        out_shape=(
            jax.ShapeDtypeStruct((images, grid_size, grid_size), WIDE),
            jax.ShapeDtypeStruct((planes, share, grid_size), WIDE),
        ),
        in_specs=[vmem] * 4 + [smem] + [vmem] * 5,
        out_specs=(vmem, vmem),
        scratch_shapes=[
            pltpu.VMEM((4, tables, grid_size), WIDE),
            pltpu.VMEM((2, images, grid_size, grid_size), WIDE),
            tuple((table, table, table) for _ in range(width)),
            pltpu.VMEM((images, grid_size, grid_size), WIDE),
            pltpu.VMEM((coefs, tables, padded, segs), WIDE),
            pltpu.VMEM((planes, padded, grid_size), WIDE),
            pltpu.VMEM((orients, padded, grid_size), WIDE),
            pltpu.VMEM((tables, coefs, padded, grid_size), WIDE),
            pltpu.VMEM((orients, coefs, padded, grid_size), WIDE),
            pltpu.VMEM((planes, coefs, padded, grid_size), WIDE),
            dma((coefs - 1,)),
            dma((coefs - 1,)),
            dma((orients - 1,)),
            dma((orients - 1,)),
            dma((coefs - 1, tables)),
            dma((coefs - 1, tables)),
            dma((orients - 1,)),
            dma((orients - 1,)),
        ],
        compiler_params=pltpu.CompilerParams(
            collective_id=0, has_side_effects=True, vmem_limit_bytes=LIMIT
        ),
    )(
        volume.reshape(images, grid_size, grid_size),
        measured[0],
        basis,
        angles,
        angle_index,
        sector_map,
        analysis,
        analysis.T,
        synthesis,
        synthesis.T,
    )
    return (gradient.reshape(volume.shape), residual[None])


def solution(mesh):
    placed = (
        P("orient", "coef", None, None),
        P("orient", None, None, None),
        P(None, None, "coef"),
        P(),
        P("orient"),
        P("orient", None),
    )
    return jax.shard_map(
        body,
        mesh=mesh,
        in_specs=placed,
        out_specs=(P("orient", "coef", None, None), P("orient", None, "coef", None)),
        check_vma=False,
    )
```

```python
import functools
import math

import jax
import jax.numpy as jnp
from jax import lax
from jax.experimental import pallas as pl
from jax.experimental.pallas import tpu as pltpu
from jax.sharding import PartitionSpec as P

WIDE = jnp.float32
NARROW = jnp.bfloat16


def dft_tables(grid_size):
    midpoint = grid_size // 2
    row_ids = jnp.arange(grid_size, dtype=jnp.int32)
    frequency = jnp.where(row_ids <= midpoint, row_ids, row_ids - midpoint)
    positions = jnp.arange(grid_size, dtype=jnp.int32)
    products = frequency[:, None] * positions[None, :] % grid_size
    radians = products.astype(jnp.float32) * (2.0 * math.pi / grid_size)
    base_wave = jnp.where((row_ids > midpoint)[:, None], jnp.sin(radians), jnp.cos(radians))
    weights = jnp.where(
        (row_ids == 0) | (row_ids == midpoint), 1.0 / grid_size, 2.0 / grid_size
    ).astype(jnp.float32)
    return (base_wave.astype(jnp.bfloat16), (base_wave * weights[:, None]).astype(jnp.bfloat16))


def cmul(left, right):
    return (
        left[0] * right[0] - left[1] * right[1],
        left[0] * right[1] + left[1] * right[0],
    )


def power_rows(base, bits, rows, lanes):
    ids = lax.broadcasted_iota(jnp.int32, (rows, lanes), 0)
    result = None
    for bit in range(bits):
        on = (ids // (1 << bit)) % 2 == 1
        term = (jnp.where(on, base[0], 1.0), jnp.where(on, base[1], 0.0))
        result = term if result is None else cmul(result, term)
        base = cmul(base, base)
    return result, base


def unit_waves(angles, grid_size, unit_ref):
    half = grid_size // 2
    count = angles.shape[0]
    lanes = lax.broadcasted_iota(jnp.int32, (count, grid_size), 1)
    frequency = jnp.where(lanes <= half, lanes, lanes - half).astype(WIDE)
    unit = 2.0 * math.pi / grid_size
    slope_rows = -jnp.sin(angles * 0.5) / jnp.cos(angles * 0.5)
    row_phase = slope_rows * frequency * unit
    col_phase = jnp.sin(angles) * (lanes - half).astype(WIDE) * unit
    unit_ref[0] = jnp.cos(row_phase)
    unit_ref[1] = jnp.sin(row_phase)
    unit_ref[2] = jnp.cos(col_phase)
    unit_ref[3] = jnp.sin(col_phase)


def build_tables(which, grid_size, unit_ref, row_ref, col_ref, mix_ref, slot, synthesis):
    half = grid_size // 2
    lanes = lax.broadcasted_iota(jnp.int32, (8, grid_size), 1)
    sign = jnp.where(lanes > half, 1.0, jnp.where((lanes > 0) & (lanes < half), -1.0, 0.0))
    coarse_count = grid_size // 8
    bits = coarse_count.bit_length() - 1

    def take(at):
        return unit_ref[at, pl.ds(which, 1), :]

    fine, eighth = power_rows((take(0), take(1)), 3, 8, grid_size)
    coarse, top = power_rows(eighth, bits, coarse_count, grid_size)
    middle = (coarse[0][half // 8 : half // 8 + 1], coarse[1][half // 8 : half // 8 + 1])
    coarse = cmul(coarse, (middle[0], -middle[1]))
    for j in range(coarse_count):
        wave = cmul((coarse[0][j : j + 1], coarse[1][j : j + 1]), fine)
        row_ref[slot, 0, 8 * j : 8 * j + 8, :] = wave[0]
        row_ref[slot, 1, 8 * j : 8 * j + 8, :] = wave[1] * sign
    for part in range(2):
        mix_ref[slot, part] = jnp.dot(
            synthesis, row_ref[slot, part].astype(NARROW), preferred_element_type=WIDE
        )
    fine, eighth = power_rows((take(2), take(3)), 3, 8, grid_size)
    coarse, highest = power_rows(eighth, bits - 1, coarse_count // 2, grid_size)
    first = lax.broadcasted_iota(jnp.int32, (8, grid_size), 0) == 0
    for j in range(coarse_count // 2):
        wave = cmul((coarse[0][j : j + 1], coarse[1][j : j + 1]), fine)
        col_ref[slot, 0, 8 * j : 8 * j + 8, :] = wave[0]
        col_ref[slot, 1, 8 * j : 8 * j + 8, :] = -wave[1]
        low = wave[0] if j else jnp.where(first, highest[0], wave[0])
        col_ref[slot, 0, half + 8 * j : half + 8 * j + 8, :] = low
        col_ref[slot, 1, half + 8 * j : half + 8 * j + 8, :] = wave[1]


def swap_rows(field):
    half = field.shape[0] // 2
    return jnp.concatenate([field[half:], field[:half]], axis=0)


def mul(left, right):
    return jnp.dot(left, right, preferred_element_type=WIDE)


def image_groups(count, width=2):
    return [range(at, min(at + width, count)) for at in range(0, count, width)]


def volume_spectra(volume_ref, analysis_t, spec_ref, images, grid_size):
    for image in range(images):
        spectrum = mul(volume_ref[image], analysis_t)
        spec_ref[0, image] = spectrum
        spec_ref[1, image] = pltpu.roll(spectrum, grid_size // 2, 1)


def forward_pair(slot, images, grid_size, spec_ref, sides, waves):
    analysis, analysis_t, synthesis = waves
    half = grid_size // 2
    sums, rolled = [[] for _ in sides], [[] for _ in sides]
    for group in image_groups(images):
        spectra = []
        for row_ref, _, _ in sides:
            fields = []
            for image in group:
                turned = (
                    spec_ref[0, image] * row_ref[slot, 0] + spec_ref[1, image] * row_ref[slot, 1]
                )
                fields.append(mul(turned.astype(NARROW), synthesis).astype(NARROW))
            spectra.append(mul(analysis, jnp.concatenate(fields, axis=1)))
        for side, (_, col_ref, mix_ref) in enumerate(sides):
            for at in range(len(group)):
                own = spectra[side][:, at * grid_size : (at + 1) * grid_size]
                turned = own * col_ref[slot, 0] + swap_rows(own) * col_ref[slot, 1]
                last = mul(turned.astype(NARROW), analysis_t)
                sums[side].append(jnp.sum(last * mix_ref[slot, 0], axis=0, keepdims=True))
                rolled[side].append(jnp.sum(last * mix_ref[slot, 1], axis=0, keepdims=True))
    profiles = []
    for side in range(len(sides)):
        total = jnp.concatenate(sums[side], axis=0)
        crossed = pltpu.roll(jnp.concatenate(rolled[side], axis=0), half, 1)
        summed = (total - crossed).astype(NARROW)
        profiles.append(mul(summed, synthesis) * (1.0 / math.sqrt(grid_size)))
    return profiles


def backward_pair(slot, spectra, images, grid_size, total_ref, sides, waves):
    analysis, analysis_t, synthesis_t = waves
    half = grid_size // 2
    for group in image_groups(images):
        spread_out = []
        for (own_rows, crossed), (_, col_ref, mix_ref) in zip(spectra, sides):
            fields = []
            for image in group:
                spread = (
                    own_rows[image : image + 1] * mix_ref[slot, 0]
                    - crossed[image : image + 1] * mix_ref[slot, 1]
                )
                own = mul(spread.astype(NARROW), analysis)
                turned = own * col_ref[slot, 0] - swap_rows(own) * col_ref[slot, 1]
                fields.append(turned.astype(NARROW))
            spread_out.append(mul(analysis_t, jnp.concatenate(fields, axis=1)).astype(NARROW))
        for at, image in enumerate(group):
            added = None
            for field, (row_ref, _, _) in zip(spread_out, sides):
                own = mul(field[:, at * grid_size : (at + 1) * grid_size], synthesis_t)
                turned = own * row_ref[slot, 0] - pltpu.roll(own, half, 1) * row_ref[slot, 1]
                added = turned if added is None else added + turned
            total_ref[image] += added


def split(value):
    high = value.astype(NARROW)
    return high, (value - high.astype(WIDE)).astype(NARROW)


MESH = pl.DeviceIdType.MESH
LIMIT = 63 << 20


def exact(left, right, contract=((1,), (0,))):
    return lax.dot_general(
        left, right, (contract, ((), ())), precision=lax.Precision.HIGHEST, preferred_element_type=WIDE
    )


def whole_kernel(
    orients, coefs, own_coefs,
    volume_hbm, data_hbm, table_hbm, angle_ref, index_ref, map_hbm, ana_ref, ana_t_ref, syn_ref, syn_t_ref,
    grad_ref, resid_ref, volume_ref, table_ref, data_ref, map_ref, basis_ref, fetch_sem,
    unit_ref, spec_ref, sides, total_ref,
    basis_all, pull_out, pull_in, prof_all, back_out, back_in,
    basis_send, basis_recv, pull_send, pull_recv, prof_send, prof_recv, back_send, back_recv,
):
    me, mine = lax.axis_index("orient"), lax.axis_index("coef")
    images, grid_size = volume_ref.shape[0], volume_ref.shape[-1]
    tables, padded, segs = basis_ref.shape
    data_copy = pltpu.make_async_copy(data_hbm, data_ref, fetch_sem.at[0])
    map_copy = pltpu.make_async_copy(map_hbm, map_ref, fetch_sem.at[1])
    table_copy = pltpu.make_async_copy(table_hbm, table_ref, fetch_sem.at[2])
    volume_copy = pltpu.make_async_copy(volume_hbm, volume_ref, fetch_sem.at[3])
    table_copy.start()
    map_copy.start()
    volume_copy.start()
    data_copy.start()
    planes = data_ref.shape[0]
    share = resid_ref.shape[1]

    def ahead(step):
        return lax.rem(me + step, orients)

    def behind(step):
        return lax.rem(me + orients - step, orients)

    def basis_copy(step):
        return pltpu.make_async_remote_copy(
            src_ref=basis_ref, dst_ref=basis_all.at[mine],
            send_sem=basis_send.at[step - 1], recv_sem=basis_recv.at[step - 1],
            device_id=(me, lax.rem(mine + step, coefs)), device_id_type=MESH,
        )

    def prof_copy(step, which):
        return pltpu.make_async_remote_copy(
            src_ref=prof_all.at[which, mine], dst_ref=prof_all.at[which, mine],
            send_sem=prof_send.at[step - 1, which], recv_sem=prof_recv.at[step - 1, which],
            device_id=(me, lax.rem(mine + step, coefs)), device_id_type=MESH,
        )

    def pull_copy(step):
        return pltpu.make_async_remote_copy(
            src_ref=pull_out.at[ahead(step)], dst_ref=pull_in.at[me],
            send_sem=pull_send.at[step - 1], recv_sem=pull_recv.at[step - 1],
            device_id=(ahead(step), mine), device_id_type=MESH,
        )

    def back_copy(step):
        return pltpu.make_async_remote_copy(
            src_ref=back_out.at[ahead(step)], dst_ref=back_in.at[me],
            send_sem=back_send.at[step - 1], recv_sem=back_recv.at[step - 1],
            device_id=(ahead(step), mine), device_id_type=MESH,
        )

    def over_steps(action):
        def one(step, carry):
            action(step)
            return carry

        lax.fori_loop(1, orients, one, 0)

    barrier = pltpu.get_barrier_semaphore()
    over_steps(
        lambda step: pl.semaphore_signal(
            barrier, inc=1, device_id=(ahead(step), mine), device_id_type=MESH
        )
    )
    for step in range(1, coefs):
        pl.semaphore_signal(
            barrier, inc=1, device_id=(me, lax.rem(mine + step, coefs)), device_id_type=MESH
        )

    row_ids = lax.broadcasted_iota(jnp.int32, (tables, grid_size), 0)
    angles = jnp.zeros((tables, grid_size), WIDE)
    for which in range(tables):
        angles = jnp.where(row_ids == which, angle_ref[which], angles)
    unit_waves(angles, grid_size, unit_ref)
    basis_ref[...] = jnp.zeros_like(basis_ref)
    table_copy.wait()
    for coef in range(own_coefs):
        basis_ref[:, coef, :] = table_ref[coef]
    volume_copy.wait()
    volume_spectra(volume_ref, ana_t_ref[...], spec_ref, images, grid_size)
    total_ref[...] = jnp.zeros_like(total_ref)
    map_copy.wait()
    map_row = map_ref[...]
    chosen = (lax.broadcasted_iota(jnp.int32, (segs, segs), 0) == map_row).astype(WIDE)
    index = index_ref[0]
    own_mix_t = exact(basis_ref[index], chosen)
    tag_row = lax.broadcasted_iota(jnp.int32, (padded, grid_size), 0) == own_coefs
    tag = index.astype(WIDE)

    data_copy.wait()
    mix_parts = jnp.concatenate(split(own_mix_t), axis=0)

    def pull_one(plane, carry):
        both = mul(mix_parts, data_ref[plane].astype(NARROW))
        pull_out[plane] = jnp.where(tag_row, tag, both[:padded] + both[padded:])
        return carry

    lax.fori_loop(0, planes, pull_one, 0, unroll=8)
    pull_in[me] = pull_out[me]
    basis_all[mine] = basis_ref[...]
    pl.semaphore_wait(barrier, orients + coefs - 2)
    for step in range(1, coefs):
        basis_copy(step).start()
    over_steps(lambda step: pull_copy(step).start())

    filler = jnp.zeros((padded - images, grid_size), WIDE)

    width = len(sides)
    pairs = tables // width

    def project(slot, carry):
        for side, refs in enumerate(sides):
            build_tables(width * slot + side, grid_size, unit_ref, *refs, slot, syn_ref[...])
        waves = (ana_ref[...], ana_t_ref[...], syn_ref[...])
        profiles = forward_pair(slot, images, grid_size, spec_ref, sides, waves)
        for side, rows in enumerate(profiles):
            prof_all[width * slot + side, mine] = jnp.concatenate([rows, filler], axis=0)
        for side in range(width):
            for step in range(1, coefs):
                prof_copy(step, width * slot + side).start()
        return carry

    lax.fori_loop(0, pairs, project, 0)

    for step in range(1, coefs):
        basis_copy(step).wait()
    over_steps(lambda step: pull_copy(step).wait())

    def arrived(slot, carry):
        for side in range(width):
            for step in range(1, coefs):
                prof_copy(step, width * slot + side).wait()
        return carry

    def contract(slot):
        found = []
        for side in range(width):
            which = width * slot + side
            rows = jnp.zeros((padded, grid_size), WIDE)
            for orient in range(orients):
                block = pull_in[orient]
                tags = block[own_coefs : own_coefs + 1]
                rows = rows - jnp.where(tags == lax.convert_element_type(which, WIDE), block, 0.0)
            for part in range(coefs):
                gram = exact(basis_ref[which], basis_all[part, which], ((1,), (1,)))
                rows = rows + exact(gram, prof_all[which, part])
            spectra = mul(rows.astype(NARROW), syn_t_ref[...]) * (1.0 / math.sqrt(grid_size))
            found.append((spectra, pltpu.roll(spectra, grid_size // 2, 1)))
        return tuple(found)

    def spread_back(slot, spectra):
        waves = (ana_ref[...], ana_t_ref[...], syn_t_ref[...])
        following = contract(jnp.minimum(slot + 1, pairs - 1))
        backward_pair(slot, spectra, images, grid_size, total_ref, sides, waves)
        return following

    def first_part(slot, spectra):
        arrived(slot + 1, 0)
        return spread_back(slot, spectra)

    early = pairs // 2
    arrived(0, 0)
    spectra = lax.fori_loop(0, early, first_part, contract(jnp.int32(0)))
    lax.fori_loop(early + 1, pairs, arrived, 0)

    def return_one(orient, carry):
        tags = pull_in[orient][own_coefs : own_coefs + 1]

        def add(which, found):
            return found + jnp.where(tags[None] == which.astype(WIDE), prof_all[which], 0.0)

        back_out[orient] = lax.fori_loop(
            0, tables, add, jnp.zeros((coefs, padded, grid_size), WIDE), unroll=16
        )
        return carry

    lax.fori_loop(0, orients, return_one, 0)
    back_in[me] = back_out[me]
    over_steps(lambda step: back_copy(step).start())
    lax.fori_loop(early, pairs, spread_back, spectra)
    for image in range(images):
        grad_ref[image] = mul(total_ref[image].astype(NARROW), ana_ref[...])

    row_ids = lax.broadcasted_iota(jnp.int32, (share, segs), 0) + mine * share
    lane_ids = lax.broadcasted_iota(jnp.int32, (share, segs), 1)
    map_column = jnp.sum(
        jnp.where(row_ids == lane_ids, map_row.astype(WIDE), 0.0), axis=1, keepdims=True
    )
    picked = (lane_ids.astype(WIDE) == map_column).astype(WIDE)
    all_basis = jnp.concatenate([basis_all[part, index] for part in range(coefs)], axis=0)
    high, low = split(exact(picked, all_basis, ((1,), (1,))))
    share_mix = jnp.concatenate([high, low, high], axis=1)
    start = pl.multiple_of(mine * share, share)
    over_steps(lambda step: back_copy(step).wait())

    def residual_one(plane, carry):
        rows = back_in[plane].reshape(coefs * padded, grid_size)
        high, low = split(rows)
        signals = mul(share_mix, jnp.concatenate([high, high, low], axis=0))
        resid_ref[plane] = signals - data_ref[plane, pl.ds(start, share), :]
        return carry

    lax.fori_loop(0, planes, residual_one, 0, unroll=8)


def body(volume, measured, basis_table, angle_table, angle_index, sector_map):
    grid_size = volume.shape[-1]
    images = volume.shape[0] * volume.shape[1]
    own_coefs = basis_table.shape[2]
    tables = angle_table.shape[0]
    planes, segs = measured.shape[1], measured.shape[2]
    orients, coefs = lax.axis_size("orient"), lax.axis_size("coef")
    share = segs // coefs
    padded = (own_coefs + 8) // 8 * 8
    analysis, synthesis = dft_tables(grid_size)
    far = pl.BlockSpec(memory_space=pltpu.HBM)
    vmem = pl.BlockSpec(memory_space=pltpu.VMEM)
    smem = pl.BlockSpec(memory_space=pltpu.SMEM)
    width = math.gcd(tables, 4)
    table = pltpu.VMEM((tables // width, 2, grid_size, grid_size), WIDE)
    dma = pltpu.SemaphoreType.DMA
    gradient, residual = pl.pallas_call(
        functools.partial(whole_kernel, orients, coefs, own_coefs),
        out_shape=(
            jax.ShapeDtypeStruct((images, grid_size, grid_size), WIDE),
            jax.ShapeDtypeStruct((planes, share, grid_size), WIDE),
        ),
        in_specs=[far, far, far, smem, smem, far] + [vmem] * 4,
        out_specs=(vmem, vmem),
        scratch_shapes=[
            pltpu.VMEM((images, grid_size, grid_size), NARROW),
            pltpu.VMEM((own_coefs, tables, segs), WIDE),
            pltpu.VMEM((planes, segs, grid_size), WIDE),
            pltpu.VMEM((1, segs), jnp.int32),
            pltpu.VMEM((tables, padded, segs), WIDE),
            dma((4,)),
            pltpu.VMEM((4, tables, grid_size), WIDE),
            pltpu.VMEM((2, images, grid_size, grid_size), WIDE),
            tuple((table, table, table) for _ in range(width)),
            pltpu.VMEM((images, grid_size, grid_size), WIDE),
            pltpu.VMEM((coefs, tables, padded, segs), WIDE),
            pltpu.VMEM((planes, padded, grid_size), WIDE),
            pltpu.VMEM((orients, padded, grid_size), WIDE),
            pltpu.VMEM((tables, coefs, padded, grid_size), WIDE),
            pltpu.VMEM((orients, coefs, padded, grid_size), WIDE),
            pltpu.VMEM((planes, coefs, padded, grid_size), WIDE),
            dma((coefs - 1,)),
            dma((coefs - 1,)),
            dma((orients - 1,)),
            dma((orients - 1,)),
            dma((coefs - 1, tables)),
            dma((coefs - 1, tables)),
            dma((orients - 1,)),
            dma((orients - 1,)),
        ],
        compiler_params=pltpu.CompilerParams(
            collective_id=0, has_side_effects=True, vmem_limit_bytes=LIMIT
        ),
    )(
        volume.reshape(images, grid_size, grid_size),
        measured[0],
        basis_table.transpose(2, 0, 1),
        angle_table,
        angle_index,
        sector_map,
        analysis,
        analysis.T,
        synthesis,
        synthesis.T,
    )
    return (gradient.reshape(volume.shape), residual[None])


def solution(mesh):
    placed = (
        P("orient", "coef", None, None),
        P("orient", None, None, None),
        P(None, None, "coef"),
        P(),
        P("orient"),
        P("orient", None),
    )
    return jax.shard_map(
        body,
        mesh=mesh,
        in_specs=placed,
        out_specs=(P("orient", "coef", None, None), P("orient", None, "coef", None)),
        check_vma=False,
    )
```

```python
import functools
import math

import jax
import jax.numpy as jnp
from jax import lax
from jax.experimental import pallas as pl
from jax.experimental.pallas import tpu as pltpu
from jax.sharding import PartitionSpec as P

WIDE = jnp.float32
NARROW = jnp.bfloat16


def dft_tables(grid_size):
    midpoint = grid_size // 2
    row_ids = jnp.arange(grid_size, dtype=jnp.int32)
    frequency = jnp.where(row_ids <= midpoint, row_ids, row_ids - midpoint)
    positions = jnp.arange(grid_size, dtype=jnp.int32)
    products = frequency[:, None] * positions[None, :] % grid_size
    radians = products.astype(jnp.float32) * (2.0 * math.pi / grid_size)
    base_wave = jnp.where((row_ids > midpoint)[:, None], jnp.sin(radians), jnp.cos(radians))
    weights = jnp.where(
        (row_ids == 0) | (row_ids == midpoint), 1.0 / grid_size, 2.0 / grid_size
    ).astype(jnp.float32)
    return (base_wave.astype(jnp.bfloat16), (base_wave * weights[:, None]).astype(jnp.bfloat16))


def cmul(left, right):
    return (
        left[0] * right[0] - left[1] * right[1],
        left[0] * right[1] + left[1] * right[0],
    )


def power_rows(base, bits, rows, lanes):
    ids = lax.broadcasted_iota(jnp.int32, (rows, lanes), 0)
    result = None
    for bit in range(bits):
        on = (ids // (1 << bit)) % 2 == 1
        term = (jnp.where(on, base[0], 1.0), jnp.where(on, base[1], 0.0))
        result = term if result is None else cmul(result, term)
        base = cmul(base, base)
    return result, base


def unit_waves(angles, grid_size, unit_ref):
    half = grid_size // 2
    count = angles.shape[0]
    lanes = lax.broadcasted_iota(jnp.int32, (count, grid_size), 1)
    frequency = jnp.where(lanes <= half, lanes, lanes - half).astype(WIDE)
    unit = 2.0 * math.pi / grid_size
    slope_rows = -jnp.sin(angles * 0.5) / jnp.cos(angles * 0.5)
    row_phase = slope_rows * frequency * unit
    col_phase = jnp.sin(angles) * (lanes - half).astype(WIDE) * unit
    unit_ref[0] = jnp.cos(row_phase)
    unit_ref[1] = jnp.sin(row_phase)
    unit_ref[2] = jnp.cos(col_phase)
    unit_ref[3] = jnp.sin(col_phase)


def build_tables(which, grid_size, unit_ref, row_ref, col_ref, mix_ref, slot, synthesis):
    half = grid_size // 2
    lanes = lax.broadcasted_iota(jnp.int32, (8, grid_size), 1)
    sign = jnp.where(lanes > half, 1.0, jnp.where((lanes > 0) & (lanes < half), -1.0, 0.0))
    coarse_count = grid_size // 8
    bits = coarse_count.bit_length() - 1

    def take(at):
        return unit_ref[at, pl.ds(which, 1), :]

    fine, eighth = power_rows((take(0), take(1)), 3, 8, grid_size)
    coarse, top = power_rows(eighth, bits, coarse_count, grid_size)
    middle = (coarse[0][half // 8 : half // 8 + 1], coarse[1][half // 8 : half // 8 + 1])
    coarse = cmul(coarse, (middle[0], -middle[1]))
    for j in range(coarse_count):
        wave = cmul((coarse[0][j : j + 1], coarse[1][j : j + 1]), fine)
        row_ref[slot, 0, 8 * j : 8 * j + 8, :] = wave[0]
        row_ref[slot, 1, 8 * j : 8 * j + 8, :] = wave[1] * sign
    for part in range(2):
        mix_ref[slot, part] = jnp.dot(
            synthesis, row_ref[slot, part].astype(NARROW), preferred_element_type=WIDE
        )
    fine, eighth = power_rows((take(2), take(3)), 3, 8, grid_size)
    coarse, highest = power_rows(eighth, bits - 1, coarse_count // 2, grid_size)
    first = lax.broadcasted_iota(jnp.int32, (8, grid_size), 0) == 0
    for j in range(coarse_count // 2):
        wave = cmul((coarse[0][j : j + 1], coarse[1][j : j + 1]), fine)
        col_ref[slot, 0, 8 * j : 8 * j + 8, :] = wave[0]
        col_ref[slot, 1, 8 * j : 8 * j + 8, :] = -wave[1]
        low = wave[0] if j else jnp.where(first, highest[0], wave[0])
        col_ref[slot, 0, half + 8 * j : half + 8 * j + 8, :] = low
        col_ref[slot, 1, half + 8 * j : half + 8 * j + 8, :] = wave[1]


def swap_rows(field):
    half = field.shape[0] // 2
    return jnp.concatenate([field[half:], field[:half]], axis=0)


def mul(left, right):
    return jnp.dot(left, right, preferred_element_type=WIDE)


def image_groups(count, width=2):
    return [range(at, min(at + width, count)) for at in range(0, count, width)]


def volume_spectra(volume_ref, analysis_t, spec_ref, images, grid_size):
    for image in range(images):
        spectrum = mul(volume_ref[image], analysis_t)
        spec_ref[0, image] = spectrum
        spec_ref[1, image] = pltpu.roll(spectrum, grid_size // 2, 1)


def forward_pair(slot, images, grid_size, spec_ref, sides, waves):
    analysis, analysis_t, synthesis = waves
    half = grid_size // 2
    sums, rolled = [[] for _ in sides], [[] for _ in sides]
    for group in image_groups(images):
        spectra = []
        for row_ref, _, _ in sides:
            fields = []
            for image in group:
                turned = (
                    spec_ref[0, image] * row_ref[slot, 0] + spec_ref[1, image] * row_ref[slot, 1]
                )
                fields.append(mul(turned.astype(NARROW), synthesis).astype(NARROW))
            spectra.append(mul(analysis, jnp.concatenate(fields, axis=1)))
        for side, (_, col_ref, mix_ref) in enumerate(sides):
            for at in range(len(group)):
                own = spectra[side][:, at * grid_size : (at + 1) * grid_size]
                turned = own * col_ref[slot, 0] + swap_rows(own) * col_ref[slot, 1]
                last = mul(turned.astype(NARROW), analysis_t)
                sums[side].append(jnp.sum(last * mix_ref[slot, 0], axis=0, keepdims=True))
                rolled[side].append(jnp.sum(last * mix_ref[slot, 1], axis=0, keepdims=True))
    profiles = []
    for side in range(len(sides)):
        total = jnp.concatenate(sums[side], axis=0)
        crossed = pltpu.roll(jnp.concatenate(rolled[side], axis=0), half, 1)
        summed = (total - crossed).astype(NARROW)
        profiles.append(mul(summed, synthesis) * (1.0 / math.sqrt(grid_size)))
    return profiles


def backward_pair(slot, spectra, images, grid_size, total_ref, sides, waves):
    analysis, analysis_t, synthesis_t = waves
    half = grid_size // 2
    for group in image_groups(images):
        spread_out = []
        for (own_rows, crossed), (_, col_ref, mix_ref) in zip(spectra, sides):
            fields = []
            for image in group:
                spread = (
                    own_rows[image : image + 1] * mix_ref[slot, 0]
                    - crossed[image : image + 1] * mix_ref[slot, 1]
                )
                own = mul(spread.astype(NARROW), analysis)
                turned = own * col_ref[slot, 0] - swap_rows(own) * col_ref[slot, 1]
                fields.append(turned.astype(NARROW))
            spread_out.append(mul(analysis_t, jnp.concatenate(fields, axis=1)).astype(NARROW))
        for at, image in enumerate(group):
            added = None
            for field, (row_ref, _, _) in zip(spread_out, sides):
                own = mul(field[:, at * grid_size : (at + 1) * grid_size], synthesis_t)
                turned = own * row_ref[slot, 0] - pltpu.roll(own, half, 1) * row_ref[slot, 1]
                added = turned if added is None else added + turned
            total_ref[image] += added


def split(value):
    high = value.astype(NARROW)
    return high, (value - high.astype(WIDE)).astype(NARROW)


MESH = pl.DeviceIdType.MESH
LIMIT = 63 << 20


def exact(left, right, contract=((1,), (0,))):
    return lax.dot_general(
        left, right, (contract, ((), ())), precision=lax.Precision.HIGHEST, preferred_element_type=WIDE
    )


def whole_kernel(
    orients, coefs, own_coefs,
    volume_hbm, data_hbm, table_hbm, angle_ref, index_ref, map_hbm, ana_ref, ana_t_ref, syn_ref, syn_t_ref,
    grad_ref, resid_ref, volume_ref, table_ref, data_ref, map_ref, basis_ref, fetch_sem,
    unit_ref, spec_ref, sides, total_ref,
    basis_all, pull_out, pull_in, prof_all, back_out, back_in,
    basis_send, basis_recv, pull_send, pull_recv, prof_send, prof_recv, back_send, back_recv,
):
    me, mine = lax.axis_index("orient"), lax.axis_index("coef")
    images, grid_size = volume_ref.shape[0], volume_ref.shape[-1]
    tables, padded, segs = basis_ref.shape
    data_copy = pltpu.make_async_copy(data_hbm, data_ref, fetch_sem.at[0])
    map_copy = pltpu.make_async_copy(map_hbm, map_ref, fetch_sem.at[1])
    table_copy = pltpu.make_async_copy(table_hbm, table_ref, fetch_sem.at[2])
    volume_copy = pltpu.make_async_copy(volume_hbm, volume_ref, fetch_sem.at[3])
    table_copy.start()
    map_copy.start()
    volume_copy.start()
    data_copy.start()
    planes = data_ref.shape[0]
    share = resid_ref.shape[1]

    def ahead(step):
        return lax.rem(me + step, orients)

    def behind(step):
        return lax.rem(me + orients - step, orients)

    def basis_copy(step):
        return pltpu.make_async_remote_copy(
            src_ref=basis_ref, dst_ref=basis_all.at[mine],
            send_sem=basis_send.at[step - 1], recv_sem=basis_recv.at[step - 1],
            device_id=(me, lax.rem(mine + step, coefs)), device_id_type=MESH,
        )

    def prof_copy(step, which):
        return pltpu.make_async_remote_copy(
            src_ref=prof_all.at[which, mine], dst_ref=prof_all.at[which, mine],
            send_sem=prof_send.at[step - 1, which], recv_sem=prof_recv.at[step - 1, which],
            device_id=(me, lax.rem(mine + step, coefs)), device_id_type=MESH,
        )

    def pull_copy(step):
        return pltpu.make_async_remote_copy(
            src_ref=pull_out.at[ahead(step)], dst_ref=pull_in.at[me],
            send_sem=pull_send.at[step - 1], recv_sem=pull_recv.at[step - 1],
            device_id=(ahead(step), mine), device_id_type=MESH,
        )

    def back_copy(step):
        return pltpu.make_async_remote_copy(
            src_ref=back_out.at[ahead(step)], dst_ref=back_in.at[me],
            send_sem=back_send.at[step - 1], recv_sem=back_recv.at[step - 1],
            device_id=(ahead(step), mine), device_id_type=MESH,
        )

    def over_steps(action):
        def one(step, carry):
            action(step)
            return carry

        lax.fori_loop(1, orients, one, 0)

    barrier = pltpu.get_barrier_semaphore()
    over_steps(
        lambda step: pl.semaphore_signal(
            barrier, inc=1, device_id=(ahead(step), mine), device_id_type=MESH
        )
    )
    for step in range(1, coefs):
        pl.semaphore_signal(
            barrier, inc=1, device_id=(me, lax.rem(mine + step, coefs)), device_id_type=MESH
        )

    row_ids = lax.broadcasted_iota(jnp.int32, (tables, grid_size), 0)
    angles = jnp.zeros((tables, grid_size), WIDE)
    for which in range(tables):
        angles = jnp.where(row_ids == which, angle_ref[which], angles)
    unit_waves(angles, grid_size, unit_ref)
    basis_ref[...] = jnp.zeros_like(basis_ref)
    table_copy.wait()
    for coef in range(own_coefs):
        basis_ref[:, coef, :] = table_ref[coef]
    volume_copy.wait()
    volume_spectra(volume_ref, ana_t_ref[...], spec_ref, images, grid_size)
    total_ref[...] = jnp.zeros_like(total_ref)
    map_copy.wait()
    map_row = map_ref[...]
    chosen = (lax.broadcasted_iota(jnp.int32, (segs, segs), 0) == map_row).astype(WIDE)
    index = index_ref[0]
    own_mix_t = exact(basis_ref[index], chosen)
    tag_row = lax.broadcasted_iota(jnp.int32, (padded, grid_size), 0) == own_coefs
    tag = index.astype(WIDE)

    data_copy.wait()
    mix_parts = jnp.concatenate(split(own_mix_t), axis=0)

    def pull_one(plane, carry):
        both = mul(mix_parts, data_ref[plane].astype(NARROW))
        pull_out[plane] = jnp.where(tag_row, tag, both[:padded] + both[padded:])
        return carry

    lax.fori_loop(0, planes, pull_one, 0, unroll=8)
    pull_in[me] = pull_out[me]
    basis_all[mine] = basis_ref[...]
    pl.semaphore_wait(barrier, orients + coefs - 2)
    for step in range(1, coefs):
        basis_copy(step).start()
    over_steps(lambda step: pull_copy(step).start())

    filler = jnp.zeros((padded - images, grid_size), WIDE)

    width = len(sides)
    pairs = tables // width

    def project(slot, carry):
        for side, refs in enumerate(sides):
            build_tables(width * slot + side, grid_size, unit_ref, *refs, slot, syn_ref[...])
        waves = (ana_ref[...], ana_t_ref[...], syn_ref[...])
        profiles = forward_pair(slot, images, grid_size, spec_ref, sides, waves)
        for side, rows in enumerate(profiles):
            prof_all[width * slot + side, mine] = jnp.concatenate([rows, filler], axis=0)
        for side in range(width):
            for step in range(1, coefs):
                prof_copy(step, width * slot + side).start()
        return carry

    lax.fori_loop(0, pairs, project, 0)

    for step in range(1, coefs):
        basis_copy(step).wait()
    over_steps(lambda step: pull_copy(step).wait())

    def arrived(slot, carry):
        for side in range(width):
            for step in range(1, coefs):
                prof_copy(step, width * slot + side).wait()
        return carry

    def contract(slot):
        found = []
        for side in range(width):
            which = width * slot + side
            rows = jnp.zeros((padded, grid_size), WIDE)
            for orient in range(orients):
                block = pull_in[orient]
                tags = block[own_coefs : own_coefs + 1]
                rows = rows - jnp.where(tags == lax.convert_element_type(which, WIDE), block, 0.0)
            for part in range(coefs):
                gram = exact(basis_ref[which], basis_all[part, which], ((1,), (1,)))
                rows = rows + exact(gram, prof_all[which, part])
            spectra = mul(rows.astype(NARROW), syn_t_ref[...]) * (1.0 / math.sqrt(grid_size))
            found.append((spectra, pltpu.roll(spectra, grid_size // 2, 1)))
        return tuple(found)

    def spread_back(slot, spectra):
        waves = (ana_ref[...], ana_t_ref[...], syn_t_ref[...])
        following = contract(jnp.minimum(slot + 1, pairs - 1))
        backward_pair(slot, spectra, images, grid_size, total_ref, sides, waves)
        return following

    def first_part(slot, spectra):
        arrived(slot + 1, 0)
        return spread_back(slot, spectra)

    early = pairs // 2
    arrived(0, 0)
    spectra = lax.fori_loop(0, early, first_part, contract(jnp.int32(0)))
    lax.fori_loop(early + 1, pairs, arrived, 0)

    def return_one(orient, carry):
        tags = pull_in[orient][own_coefs : own_coefs + 1]

        def add(which, found):
            return found + jnp.where(tags[None] == which.astype(WIDE), prof_all[which], 0.0)

        back_out[orient] = lax.fori_loop(
            0, tables, add, jnp.zeros((coefs, padded, grid_size), WIDE), unroll=16
        )
        return carry

    lax.fori_loop(0, orients, return_one, 0)
    back_in[me] = back_out[me]
    over_steps(lambda step: back_copy(step).start())
    lax.fori_loop(early, pairs, spread_back, spectra)
    for image in range(images):
        grad_ref[image] = mul(total_ref[image].astype(NARROW), ana_ref[...])

    row_ids = lax.broadcasted_iota(jnp.int32, (share, segs), 0) + mine * share
    lane_ids = lax.broadcasted_iota(jnp.int32, (share, segs), 1)
    map_column = jnp.sum(
        jnp.where(row_ids == lane_ids, map_row.astype(WIDE), 0.0), axis=1, keepdims=True
    )
    picked = (lane_ids.astype(WIDE) == map_column).astype(WIDE)
    all_basis = jnp.concatenate([basis_all[part, index] for part in range(coefs)], axis=0)
    high, low = split(exact(picked, all_basis, ((1,), (1,))))
    share_mix = jnp.concatenate([high, low, high], axis=1)
    start = pl.multiple_of(mine * share, share)
    over_steps(lambda step: back_copy(step).wait())

    def residual_one(plane, carry):
        rows = back_in[plane].reshape(coefs * padded, grid_size)
        high, low = split(rows)
        signals = mul(share_mix, jnp.concatenate([high, high, low], axis=0))
        resid_ref[plane] = signals - data_ref[plane, pl.ds(start, share), :]
        return carry

    lax.fori_loop(0, planes, residual_one, 0, unroll=8)


def body(volume, measured, basis_table, angle_table, angle_index, sector_map):
    grid_size = volume.shape[-1]
    images = volume.shape[0] * volume.shape[1]
    own_coefs = basis_table.shape[2]
    tables = angle_table.shape[0]
    planes, segs = measured.shape[1], measured.shape[2]
    orients, coefs = lax.axis_size("orient"), lax.axis_size("coef")
    share = segs // coefs
    padded = (own_coefs + 8) // 8 * 8
    analysis, synthesis = dft_tables(grid_size)
    far = pl.BlockSpec(memory_space=pltpu.HBM)
    vmem = pl.BlockSpec(memory_space=pltpu.VMEM)
    smem = pl.BlockSpec(memory_space=pltpu.SMEM)
    width = math.gcd(tables, 8)
    table = pltpu.VMEM((tables // width, 2, grid_size, grid_size), WIDE)
    dma = pltpu.SemaphoreType.DMA
    gradient, residual = pl.pallas_call(
        functools.partial(whole_kernel, orients, coefs, own_coefs),
        out_shape=(
            jax.ShapeDtypeStruct((images, grid_size, grid_size), WIDE),
            jax.ShapeDtypeStruct((planes, share, grid_size), WIDE),
        ),
        in_specs=[far, far, far, smem, smem, far] + [vmem] * 4,
        out_specs=(vmem, vmem),
        scratch_shapes=[
            pltpu.VMEM((images, grid_size, grid_size), NARROW),
            pltpu.VMEM((own_coefs, tables, segs), WIDE),
            pltpu.VMEM((planes, segs, grid_size), WIDE),
            pltpu.VMEM((1, segs), jnp.int32),
            pltpu.VMEM((tables, padded, segs), WIDE),
            dma((4,)),
            pltpu.VMEM((4, tables, grid_size), WIDE),
            pltpu.VMEM((2, images, grid_size, grid_size), WIDE),
            tuple((table, table, table) for _ in range(width)),
            pltpu.VMEM((images, grid_size, grid_size), WIDE),
            pltpu.VMEM((coefs, tables, padded, segs), WIDE),
            pltpu.VMEM((planes, padded, grid_size), WIDE),
            pltpu.VMEM((orients, padded, grid_size), WIDE),
            pltpu.VMEM((tables, coefs, padded, grid_size), WIDE),
            pltpu.VMEM((orients, coefs, padded, grid_size), WIDE),
            pltpu.VMEM((planes, coefs, padded, grid_size), WIDE),
            dma((coefs - 1,)),
            dma((coefs - 1,)),
            dma((orients - 1,)),
            dma((orients - 1,)),
            dma((coefs - 1, tables)),
            dma((coefs - 1, tables)),
            dma((orients - 1,)),
            dma((orients - 1,)),
        ],
        compiler_params=pltpu.CompilerParams(
            collective_id=0, has_side_effects=True, vmem_limit_bytes=LIMIT
        ),
    )(
        volume.reshape(images, grid_size, grid_size),
        measured[0],
        basis_table.transpose(2, 0, 1),
        angle_table,
        angle_index,
        sector_map,
        analysis,
        analysis.T,
        synthesis,
        synthesis.T,
    )
    return (gradient.reshape(volume.shape), residual[None])


def solution(mesh):
    placed = (
        P("orient", "coef", None, None),
        P("orient", None, None, None),
        P(None, None, "coef"),
        P(),
        P("orient"),
        P("orient", None),
    )
    return jax.shard_map(
        body,
        mesh=mesh,
        in_specs=placed,
        out_specs=(P("orient", "coef", None, None), P("orient", None, "coef", None)),
        check_vma=False,
    )
```

```python
import functools
import math

import jax
import jax.numpy as jnp
from jax import lax
from jax.experimental import pallas as pl
from jax.experimental.pallas import tpu as pltpu
from jax.sharding import PartitionSpec as P

WIDE = jnp.float32
NARROW = jnp.bfloat16


def dft_tables(grid_size):
    midpoint = grid_size // 2
    row_ids = jnp.arange(grid_size, dtype=jnp.int32)
    frequency = jnp.where(row_ids <= midpoint, row_ids, row_ids - midpoint)
    positions = jnp.arange(grid_size, dtype=jnp.int32)
    products = frequency[:, None] * positions[None, :] % grid_size
    radians = products.astype(jnp.float32) * (2.0 * math.pi / grid_size)
    base_wave = jnp.where((row_ids > midpoint)[:, None], jnp.sin(radians), jnp.cos(radians))
    weights = jnp.where(
        (row_ids == 0) | (row_ids == midpoint), 1.0 / grid_size, 2.0 / grid_size
    ).astype(jnp.float32)
    return (base_wave.astype(jnp.bfloat16), (base_wave * weights[:, None]).astype(jnp.bfloat16))


def cmul(left, right):
    return (
        left[0] * right[0] - left[1] * right[1],
        left[0] * right[1] + left[1] * right[0],
    )


def power_rows(base, bits, rows, lanes):
    ids = lax.broadcasted_iota(jnp.int32, (rows, lanes), 0)
    result = None
    for bit in range(bits):
        on = (ids // (1 << bit)) % 2 == 1
        term = (jnp.where(on, base[0], 1.0), jnp.where(on, base[1], 0.0))
        result = term if result is None else cmul(result, term)
        base = cmul(base, base)
    return result, base


def unit_waves(angles, grid_size, unit_ref):
    half = grid_size // 2
    count = angles.shape[0]
    lanes = lax.broadcasted_iota(jnp.int32, (count, grid_size), 1)
    frequency = jnp.where(lanes <= half, lanes, lanes - half).astype(WIDE)
    unit = 2.0 * math.pi / grid_size
    slope_rows = -jnp.sin(angles * 0.5) / jnp.cos(angles * 0.5)
    row_phase = slope_rows * frequency * unit
    col_phase = jnp.sin(angles) * (lanes - half).astype(WIDE) * unit
    unit_ref[0] = jnp.cos(row_phase)
    unit_ref[1] = jnp.sin(row_phase)
    unit_ref[2] = jnp.cos(col_phase)
    unit_ref[3] = jnp.sin(col_phase)


def build_tables(which, grid_size, unit_ref, row_ref, col_ref, mix_ref, slot, synthesis):
    half = grid_size // 2
    lanes = lax.broadcasted_iota(jnp.int32, (8, grid_size), 1)
    sign = jnp.where(lanes > half, 1.0, jnp.where((lanes > 0) & (lanes < half), -1.0, 0.0))
    coarse_count = grid_size // 8
    bits = coarse_count.bit_length() - 1

    def take(at):
        return unit_ref[at, pl.ds(which, 1), :]

    fine, eighth = power_rows((take(0), take(1)), 3, 8, grid_size)
    coarse, top = power_rows(eighth, bits, coarse_count, grid_size)
    middle = (coarse[0][half // 8 : half // 8 + 1], coarse[1][half // 8 : half // 8 + 1])
    coarse = cmul(coarse, (middle[0], -middle[1]))
    for j in range(coarse_count):
        wave = cmul((coarse[0][j : j + 1], coarse[1][j : j + 1]), fine)
        row_ref[slot, 0, 8 * j : 8 * j + 8, :] = wave[0]
        row_ref[slot, 1, 8 * j : 8 * j + 8, :] = wave[1] * sign
    for part in range(2):
        mix_ref[slot, part] = jnp.dot(
            synthesis, row_ref[slot, part].astype(NARROW), preferred_element_type=WIDE
        )
    fine, eighth = power_rows((take(2), take(3)), 3, 8, grid_size)
    coarse, highest = power_rows(eighth, bits - 1, coarse_count // 2, grid_size)
    first = lax.broadcasted_iota(jnp.int32, (8, grid_size), 0) == 0
    for j in range(coarse_count // 2):
        wave = cmul((coarse[0][j : j + 1], coarse[1][j : j + 1]), fine)
        col_ref[slot, 0, 8 * j : 8 * j + 8, :] = wave[0]
        col_ref[slot, 1, 8 * j : 8 * j + 8, :] = -wave[1]
        low = wave[0] if j else jnp.where(first, highest[0], wave[0])
        col_ref[slot, 0, half + 8 * j : half + 8 * j + 8, :] = low
        col_ref[slot, 1, half + 8 * j : half + 8 * j + 8, :] = wave[1]


def swap_rows(field):
    half = field.shape[0] // 2
    return jnp.concatenate([field[half:], field[:half]], axis=0)


def mul(left, right):
    return jnp.dot(left, right, preferred_element_type=WIDE)


def image_groups(count, width=2):
    return [range(at, min(at + width, count)) for at in range(0, count, width)]


def volume_spectra(volume_ref, analysis_t, spec_ref, images, grid_size):
    for image in range(images):
        spectrum = mul(volume_ref[image], analysis_t)
        spec_ref[0, image] = spectrum
        spec_ref[1, image] = pltpu.roll(spectrum, grid_size // 2, 1)


def forward_pair(slot, images, grid_size, spec_ref, sides, waves):
    analysis, analysis_t, synthesis = waves
    half = grid_size // 2
    sums, rolled = [[] for _ in sides], [[] for _ in sides]
    for group in image_groups(images):
        spectra = []
        for row_ref, _, _ in sides:
            fields = []
            for image in group:
                turned = (
                    spec_ref[0, image] * row_ref[slot, 0] + spec_ref[1, image] * row_ref[slot, 1]
                )
                fields.append(mul(turned.astype(NARROW), synthesis).astype(NARROW))
            spectra.append(mul(analysis, jnp.concatenate(fields, axis=1)))
        for side, (_, col_ref, mix_ref) in enumerate(sides):
            for at in range(len(group)):
                own = spectra[side][:, at * grid_size : (at + 1) * grid_size]
                turned = own * col_ref[slot, 0] + swap_rows(own) * col_ref[slot, 1]
                last = mul(turned.astype(NARROW), analysis_t)
                sums[side].append(jnp.sum(last * mix_ref[slot, 0], axis=0, keepdims=True))
                rolled[side].append(jnp.sum(last * mix_ref[slot, 1], axis=0, keepdims=True))
    profiles = []
    for side in range(len(sides)):
        total = jnp.concatenate(sums[side], axis=0)
        crossed = pltpu.roll(jnp.concatenate(rolled[side], axis=0), half, 1)
        summed = (total - crossed).astype(NARROW)
        profiles.append(mul(summed, synthesis) * (1.0 / math.sqrt(grid_size)))
    return profiles


def backward_pair(slot, spectra, images, grid_size, total_ref, sides, waves):
    analysis, analysis_t, synthesis_t = waves
    half = grid_size // 2
    for group in image_groups(images):
        spread_out = []
        for (own_rows, crossed), (_, col_ref, mix_ref) in zip(spectra, sides):
            fields = []
            for image in group:
                spread = (
                    own_rows[image : image + 1] * mix_ref[slot, 0]
                    - crossed[image : image + 1] * mix_ref[slot, 1]
                )
                own = mul(spread.astype(NARROW), analysis)
                turned = own * col_ref[slot, 0] - swap_rows(own) * col_ref[slot, 1]
                fields.append(turned.astype(NARROW))
            spread_out.append(mul(analysis_t, jnp.concatenate(fields, axis=1)).astype(NARROW))
        for at, image in enumerate(group):
            added = None
            for field, (row_ref, _, _) in zip(spread_out, sides):
                own = mul(field[:, at * grid_size : (at + 1) * grid_size], synthesis_t)
                turned = own * row_ref[slot, 0] - pltpu.roll(own, half, 1) * row_ref[slot, 1]
                added = turned if added is None else added + turned
            total_ref[image] += added


def split(value):
    high = value.astype(NARROW)
    return high, (value - high.astype(WIDE)).astype(NARROW)


MESH = pl.DeviceIdType.MESH
LIMIT = 63 << 20


def exact(left, right, contract=((1,), (0,))):
    return lax.dot_general(
        left, right, (contract, ((), ())), precision=lax.Precision.HIGHEST, preferred_element_type=WIDE
    )


def whole_kernel(
    orients, coefs, own_coefs,
    volume_hbm, data_hbm, table_hbm, angle_ref, index_ref, map_hbm, ana_ref, ana_t_ref, syn_ref, syn_t_ref,
    grad_ref, resid_ref, volume_ref, table_ref, data_ref, map_ref, basis_ref, fetch_sem,
    unit_ref, spec_ref, sides, total_ref,
    basis_all, pull_out, pull_in, prof_all, back_out, back_in,
    basis_send, basis_recv, pull_send, pull_recv, prof_send, prof_recv, back_send, back_recv,
):
    me, mine = lax.axis_index("orient"), lax.axis_index("coef")
    images, grid_size = volume_ref.shape[0], volume_ref.shape[-1]
    tables, padded, segs = basis_ref.shape
    data_copy = pltpu.make_async_copy(data_hbm, data_ref, fetch_sem.at[0])
    map_copy = pltpu.make_async_copy(map_hbm, map_ref, fetch_sem.at[1])
    table_copy = pltpu.make_async_copy(table_hbm, table_ref, fetch_sem.at[2])
    volume_copy = pltpu.make_async_copy(volume_hbm, volume_ref, fetch_sem.at[3])
    table_copy.start()
    map_copy.start()
    volume_copy.start()
    data_copy.start()
    planes = data_ref.shape[0]
    share = resid_ref.shape[1]

    def ahead(step):
        return lax.rem(me + step, orients)

    def behind(step):
        return lax.rem(me + orients - step, orients)

    def basis_copy(step):
        return pltpu.make_async_remote_copy(
            src_ref=basis_ref, dst_ref=basis_all.at[mine],
            send_sem=basis_send.at[step - 1], recv_sem=basis_recv.at[step - 1],
            device_id=(me, lax.rem(mine + step, coefs)), device_id_type=MESH,
        )

    def prof_copy(step, which):
        return pltpu.make_async_remote_copy(
            src_ref=prof_all.at[which, mine], dst_ref=prof_all.at[which, mine],
            send_sem=prof_send.at[step - 1, which], recv_sem=prof_recv.at[step - 1, which],
            device_id=(me, lax.rem(mine + step, coefs)), device_id_type=MESH,
        )

    def pull_copy(step):
        return pltpu.make_async_remote_copy(
            src_ref=pull_out.at[ahead(step)], dst_ref=pull_in.at[me],
            send_sem=pull_send.at[step - 1], recv_sem=pull_recv.at[step - 1],
            device_id=(ahead(step), mine), device_id_type=MESH,
        )

    def back_copy(step):
        return pltpu.make_async_remote_copy(
            src_ref=back_out.at[ahead(step)], dst_ref=back_in.at[me],
            send_sem=back_send.at[step - 1], recv_sem=back_recv.at[step - 1],
            device_id=(ahead(step), mine), device_id_type=MESH,
        )

    def over_steps(action):
        def one(step, carry):
            action(step)
            return carry

        lax.fori_loop(1, orients, one, 0)

    barrier = pltpu.get_barrier_semaphore()
    over_steps(
        lambda step: pl.semaphore_signal(
            barrier, inc=1, device_id=(ahead(step), mine), device_id_type=MESH
        )
    )
    for step in range(1, coefs):
        pl.semaphore_signal(
            barrier, inc=1, device_id=(me, lax.rem(mine + step, coefs)), device_id_type=MESH
        )

    row_ids = lax.broadcasted_iota(jnp.int32, (tables, grid_size), 0)
    angles = jnp.zeros((tables, grid_size), WIDE)
    for which in range(tables):
        angles = jnp.where(row_ids == which, angle_ref[which], angles)
    unit_waves(angles, grid_size, unit_ref)
    basis_ref[...] = jnp.zeros_like(basis_ref)
    table_copy.wait()
    for coef in range(own_coefs):
        basis_ref[:, coef, :] = table_ref[coef]
    volume_copy.wait()
    volume_spectra(volume_ref, ana_t_ref[...], spec_ref, images, grid_size)
    total_ref[...] = jnp.zeros_like(total_ref)
    map_copy.wait()
    map_row = map_ref[...]
    chosen = (lax.broadcasted_iota(jnp.int32, (segs, segs), 0) == map_row).astype(WIDE)
    index = index_ref[0]
    own_mix_t = exact(basis_ref[index], chosen)
    tag_row = lax.broadcasted_iota(jnp.int32, (padded, grid_size), 0) == own_coefs
    tag = index.astype(WIDE)

    data_copy.wait()
    mix_parts = jnp.concatenate(split(own_mix_t), axis=0)

    def pull_one(plane, carry):
        both = mul(mix_parts, data_ref[plane].astype(NARROW))
        pull_out[plane] = jnp.where(tag_row, tag, both[:padded] + both[padded:])
        return carry

    lax.fori_loop(0, planes, pull_one, 0, unroll=8)
    pull_in[me] = pull_out[me]
    basis_all[mine] = basis_ref[...]
    pl.semaphore_wait(barrier, orients + coefs - 2)
    for step in range(1, coefs):
        basis_copy(step).start()
    over_steps(lambda step: pull_copy(step).start())

    filler = jnp.zeros((padded - images, grid_size), WIDE)

    width = len(sides)
    pairs = tables // width

    def project(slot, carry):
        for side, refs in enumerate(sides):
            build_tables(width * slot + side, grid_size, unit_ref, *refs, slot, syn_ref[...])
        waves = (ana_ref[...], ana_t_ref[...], syn_ref[...])
        profiles = forward_pair(slot, images, grid_size, spec_ref, sides, waves)
        for side, rows in enumerate(profiles):
            prof_all[width * slot + side, mine] = jnp.concatenate([rows, filler], axis=0)
        for side in range(width):
            for step in range(1, coefs):
                prof_copy(step, width * slot + side).start()
        return carry

    lax.fori_loop(0, pairs, project, 0)

    for step in range(1, coefs):
        basis_copy(step).wait()
    over_steps(lambda step: pull_copy(step).wait())

    def arrived(slot, carry):
        for side in range(width):
            for step in range(1, coefs):
                prof_copy(step, width * slot + side).wait()
        return carry

    def contract(slot):
        found = []
        for side in range(width):
            which = width * slot + side
            rows = jnp.zeros((padded, grid_size), WIDE)
            for orient in range(orients):
                block = pull_in[orient]
                tags = block[own_coefs : own_coefs + 1]
                rows = rows - jnp.where(tags == lax.convert_element_type(which, WIDE), block, 0.0)
            for part in range(coefs):
                gram = exact(basis_ref[which], basis_all[part, which], ((1,), (1,)))
                rows = rows + exact(gram, prof_all[which, part])
            spectra = mul(rows.astype(NARROW), syn_t_ref[...]) * (1.0 / math.sqrt(grid_size))
            found.append((spectra, pltpu.roll(spectra, grid_size // 2, 1)))
        return tuple(found)

    def last_back(slot, spectra):
        waves = (ana_ref[...], ana_t_ref[...], syn_t_ref[...])
        backward_pair(slot, spectra, images, grid_size, total_ref, sides, waves)

    def spread_back(slot, spectra):
        following = contract(slot + 1)
        last_back(slot, spectra)
        return following

    def first_part(slot, spectra):
        arrived(slot + 1, 0)
        return spread_back(slot, spectra)

    early = pairs // 2
    arrived(0, 0)
    spectra = lax.fori_loop(0, early, first_part, contract(jnp.int32(0)))
    lax.fori_loop(early + 1, pairs, arrived, 0)

    def return_one(orient, carry):
        tags = pull_in[orient][own_coefs : own_coefs + 1]

        def add(which, found):
            return found + jnp.where(tags[None] == which.astype(WIDE), prof_all[which], 0.0)

        back_out[orient] = lax.fori_loop(
            0, tables, add, jnp.zeros((coefs, padded, grid_size), WIDE), unroll=16
        )
        return carry

    lax.fori_loop(0, orients, return_one, 0)
    back_in[me] = back_out[me]
    over_steps(lambda step: back_copy(step).start())
    if early < pairs - 1:
        spectra = lax.fori_loop(early, pairs - 1, spread_back, spectra)
    last_back(pairs - 1, spectra)
    for image in range(images):
        grad_ref[image] = total_ref[image].astype(NARROW)

    row_ids = lax.broadcasted_iota(jnp.int32, (share, segs), 0) + mine * share
    lane_ids = lax.broadcasted_iota(jnp.int32, (share, segs), 1)
    map_column = jnp.sum(
        jnp.where(row_ids == lane_ids, map_row.astype(WIDE), 0.0), axis=1, keepdims=True
    )
    picked = (lane_ids.astype(WIDE) == map_column).astype(WIDE)
    all_basis = jnp.concatenate([basis_all[part, index] for part in range(coefs)], axis=0)
    high, low = split(exact(picked, all_basis, ((1,), (1,))))
    share_mix = jnp.concatenate([high, low, high], axis=1)
    start = pl.multiple_of(mine * share, share)
    over_steps(lambda step: back_copy(step).wait())

    def residual_one(plane, carry):
        rows = back_in[plane].reshape(coefs * padded, grid_size)
        high, low = split(rows)
        signals = mul(share_mix, jnp.concatenate([high, high, low], axis=0))
        resid_ref[plane] = signals - data_ref[plane, pl.ds(start, share), :]
        return carry

    lax.fori_loop(0, planes, residual_one, 0, unroll=8)


def body(volume, measured, basis_table, angle_table, angle_index, sector_map):
    grid_size = volume.shape[-1]
    images = volume.shape[0] * volume.shape[1]
    own_coefs = basis_table.shape[2]
    tables = angle_table.shape[0]
    planes, segs = measured.shape[1], measured.shape[2]
    orients, coefs = lax.axis_size("orient"), lax.axis_size("coef")
    share = segs // coefs
    padded = (own_coefs + 8) // 8 * 8
    analysis, synthesis = dft_tables(grid_size)
    analysis, analysis_t, synthesis, synthesis_t = lax.optimization_barrier(
        (analysis, analysis.T, synthesis, synthesis.T)
    )
    far = pl.BlockSpec(memory_space=pltpu.HBM)
    vmem = pl.BlockSpec(memory_space=pltpu.VMEM)
    smem = pl.BlockSpec(memory_space=pltpu.SMEM)
    width = math.gcd(tables, 8)
    table = pltpu.VMEM((tables // width, 2, grid_size, grid_size), WIDE)
    dma = pltpu.SemaphoreType.DMA
    summed, residual = pl.pallas_call(
        functools.partial(whole_kernel, orients, coefs, own_coefs),
        out_shape=(
            jax.ShapeDtypeStruct((images, grid_size, grid_size), NARROW),
            jax.ShapeDtypeStruct((planes, share, grid_size), WIDE),
        ),
        in_specs=[far, far, far, smem, smem, far] + [vmem] * 4,
        out_specs=(vmem, vmem),
        scratch_shapes=[
            pltpu.VMEM((images, grid_size, grid_size), NARROW),
            pltpu.VMEM((own_coefs, tables, segs), WIDE),
            pltpu.VMEM((planes, segs, grid_size), WIDE),
            pltpu.VMEM((1, segs), jnp.int32),
            pltpu.VMEM((tables, padded, segs), WIDE),
            dma((4,)),
            pltpu.VMEM((4, tables, grid_size), WIDE),
            pltpu.VMEM((2, images, grid_size, grid_size), WIDE),
            tuple((table, table, table) for _ in range(width)),
            pltpu.VMEM((images, grid_size, grid_size), WIDE),
            pltpu.VMEM((coefs, tables, padded, segs), WIDE),
            pltpu.VMEM((planes, padded, grid_size), WIDE),
            pltpu.VMEM((orients, padded, grid_size), WIDE),
            pltpu.VMEM((tables, coefs, padded, grid_size), WIDE),
            pltpu.VMEM((orients, coefs, padded, grid_size), WIDE),
            pltpu.VMEM((planes, coefs, padded, grid_size), WIDE),
            dma((coefs - 1,)),
            dma((coefs - 1,)),
            dma((orients - 1,)),
            dma((orients - 1,)),
            dma((coefs - 1, tables)),
            dma((coefs - 1, tables)),
            dma((orients - 1,)),
            dma((orients - 1,)),
        ],
        compiler_params=pltpu.CompilerParams(
            collective_id=0, has_side_effects=True, vmem_limit_bytes=LIMIT
        ),
    )(
        volume.reshape(images, grid_size, grid_size),
        measured[0],
        basis_table.transpose(2, 0, 1),
        angle_table,
        angle_index,
        sector_map,
        analysis,
        analysis_t,
        synthesis,
        synthesis_t,
    )
    gradient = jnp.einsum("cyr,rx->cyx", summed, analysis, preferred_element_type=WIDE)
    return (gradient.reshape(volume.shape), residual[None])


def solution(mesh):
    placed = (
        P("orient", "coef", None, None),
        P("orient", None, None, None),
        P(None, None, "coef"),
        P(),
        P("orient"),
        P("orient", None),
    )
    return jax.shard_map(
        body,
        mesh=mesh,
        in_specs=placed,
        out_specs=(P("orient", "coef", None, None), P("orient", None, "coef", None)),
        check_vma=False,
    )
```
